32 devices in a mesh: dp: 8 (over y, x, core), tensor: 4 (over z).
Axes of the slice: x: 2, y: 2, z: 4, core: 2. Of those that a mesh axis runs over, the one named last changes fastest.
Arguments:
- tokens: bfloat16 [8, 1024, 2048], P('dp', None, 'tensor'), may hold values from -6 to 6
- cotangent: bfloat16 [8, 1024, 2048], P('dp', None, 'tensor'), may hold values from -6 to 6
- norm_gains: bfloat16 [2, 2048], replicated, may hold values from 0.5 to 1.5
- query_key_value_matrix: bfloat16 [3, 2048, 2048], P(None, None, 'tensor'), may hold values from -0.125 to 0.125
- output_matrix: bfloat16 [2048, 2048], P('tensor'), may hold values from -0.375 to 0.375
- gate_up_matrix: bfloat16 [2, 2048, 8192], P(None, None, 'tensor'), may hold values from -0.125 to 0.125
- down_matrix: bfloat16 [8192, 2048], P('tensor'), may hold values from -0.0625 to 0.0625
- lead_factors: bfloat16 [5, 4, 2048, 16], replicated, may hold values from -0.125 to 0.125
- head_factors: bfloat16 [3, 4, 16, 2048], P(None, None, None, 'tensor'), may hold values from -0.375 to 0.375
- unit_factors: bfloat16 [2, 4, 16, 8192], P(None, None, None, 'tensor'), may hold values from -0.375 to 0.375
- merge_factors: bfloat16 [4, 2048, 16], P(None, 'tensor'), may hold values from -0.375 to 0.375
- down_factors: bfloat16 [4, 8192, 16], P(None, 'tensor'), may hold values from -0.0625 to 0.0625
- tail_factors: bfloat16 [2, 4, 16, 2048], replicated, may hold values from -0.375 to 0.375
- doc_ids: int32 [8, 1024], P('dp'), may hold values from 0 to 127, never falling along the last dimension, each value on 1 to 512 neighbouring positions
- keep_mask: int32 [8, 1024], P('dp'), may hold values 0 or 1
- adapter_pick: int32 [8, 1], P('dp'), may hold values from 0 to 3
Outputs:
- block_output: bfloat16 [8, 1024, 2048], P('dp', None, 'tensor')
- tokens_grad: bfloat16 [8, 1024, 2048], P('dp', None, 'tensor')
- lead_grad: float32 [5, 4, 2048, 16], replicated
- head_grad: float32 [3, 4, 16, 2048], P(None, None, None, 'tensor')
- unit_grad: float32 [2, 4, 16, 8192], P(None, None, None, 'tensor')
- merge_grad: float32 [4, 2048, 16], P(None, 'tensor')
- down_grad: float32 [4, 8192, 16], P(None, 'tensor')
- tail_grad: float32 [2, 4, 16, 2048], replicated
The draws below stay inside these ranges and needn't reach their ends.
Inputs may be any that keep to these rules, and one draw needn't show every extreme that they name: `doc_ids`: ids never fall along a sequence; one document holds at most 512 tokens. `adapter_pick`: every adapter is picked by some sequence.
All inputs are finite; a program needn't handle non-finite values. No bound on the sum of `keep_mask` on one device may be relied on, other than what follows from the above.
Results may differ from the reference program's by a relative error of at most 0.017.
Values may be sent and summed in bfloat16 or wider, within the bound.
No kernel may reach another device: no remote copies, remote signals or barrier semaphores. Data moves between devices by JAX's collectives and lax.ppermute only.
A program may use at most 320 MiB of HBM per device.

```python
import math
import jax
import jax.numpy as jnp
import numpy as np
from jax import lax

D = 2048
FF = 8192
HEADS = 32
HEAD_DIM = 64
RANK = 16
ADAPTERS = 4
SEQ_LEN = 1024
SEQS = 8
N_TENSOR = 4


def set_ends(values, rng, smallest, top_value):
    longest = values.shape.index(max(values.shape))
    spots = []
    for shift in (0, 1):
        where = [jax.random.randint(jax.random.fold_in(rng, axis), (), 0, length) for axis, length in enumerate(values.shape)]
        where[longest] = (where[longest] + shift) % values.shape[longest]
        spots.append(tuple(where))
    return values.at[spots[0]].set(smallest).at[spots[1]].set(top_value)


def shard_levels(rng, extent, cuts, smallest, largest):
    factor_of, own = 1.0, jax.random.fold_in(rng, 6)
    for dim, shards_of in cuts:
        steps = jnp.exp(jax.random.uniform(jax.random.fold_in(own, dim), (shards_of,), jnp.float32, smallest / len(cuts), largest / len(cuts)))
        factor_of = factor_of * jnp.repeat(steps, extent[dim] // shards_of).reshape([-1 if axis == dim else 1 for axis in range(len(extent))])
    return factor_of


def picks_of(own_key, rows, number_of, top, lift):
    sequence = jax.random.permutation(jax.random.fold_in(own_key, 1), number_of)
    boost = sequence
    for power in range(3):
        boost = boost * boost // number_of
    boost = boost * lift // number_of
    tickets = jax.random.randint(jax.random.fold_in(own_key, 2), (rows, number_of), 0, 4096) + boost
    sure = jax.random.permutation(jax.random.fold_in(own_key, 3), rows)[jnp.arange(number_of) % rows]
    tickets = jnp.where(jnp.arange(rows)[:, None] == sure[None, :], 1 << 14, tickets)
    merit = tickets * number_of + jnp.arange(number_of)
    return lax.top_k(merit.astype(jnp.int32), top)[1].astype(jnp.int32)


def profile(number_of, total, limit, lean):
    weights = [(1 << 20) // math.isqrt(grade ** lean) + 1 for grade in range(2, number_of + 1)]
    rest, counts = total - limit - (number_of - 1), [1] * (number_of - 1)
    while rest > 0:
        candidates = [i for i in range(number_of - 1) if counts[i] < limit]
        whole, left = sum([weights[i] for i in candidates]), rest
        for i in candidates:
            addition = min(limit - counts[i], max(1, left * weights[i] // whole), rest)
            counts[i] = counts[i] + addition
            rest = rest - addition
    return np.array([limit] + counts)


def uneven_parts(key, count, total, most, slope):
    if count == 2:
        one = jax.random.randint(key, (), max(1, total - most), min(most, total - 1) + 1)
        return jnp.stack([one, total - one])
    sizes = jnp.asarray(profile(count, total, most, slope), jnp.int32)
    couples = (count - 1) // 2
    donor, receiver = sizes[1:1 + 2 * couples:2], sizes[2:2 + 2 * couples:2]
    slack = jnp.minimum(donor - 1, most - receiver)
    moved = jax.random.randint(jax.random.fold_in(key, 1), (couples,), 0, 1 << 20) % (slack + 1)
    sizes = sizes.at[1:1 + 2 * couples:2].set(donor - moved).at[2:2 + 2 * couples:2].set(receiver + moved)
    return sizes[jax.random.permutation(jax.random.fold_in(key, 2), count)]


def noise(stream_key, dims, deviation, reach, split=(), held_as=jnp.bfloat16):
    entries = jax.random.normal(stream_key, dims, jnp.float32) * deviation
    if len(split) > 0:
        entries = shard_levels(stream_key, dims, split, -0.22, 0.18) * entries
    return jnp.clip(entries, min=-reach, max=reach).astype(held_as)


def setup_inputs(seed: int = 0) -> dict:
    arg_keys = jax.random.split(jax.random.key(seed), 17)
    return {
        "tokens": noise(arg_keys[0], (SEQS, SEQ_LEN, D), 1.0, 6.0, ((0, 8), (2, 4))),
        "cotangent": noise(arg_keys[1], (SEQS, SEQ_LEN, D), 1.0, 6.0, ((0, 8), (2, 4))),
        "norm_gains": jnp.clip(1.0 + 0.1 * jax.random.normal(arg_keys[2], (2, D), jnp.float32), 0.5, 1.5).astype(jnp.bfloat16),
        "query_key_value_matrix": noise(arg_keys[3], (3, D, D), D ** -0.5, 0.125, ((2, 4),)),
        "output_matrix": noise(arg_keys[4], (D, D), (D // 8) ** -0.5, 0.375, ((0, 4),)),
        "gate_up_matrix": noise(arg_keys[5], (2, D, FF), D ** -0.5, 0.125, ((2, 4),)),
        "down_matrix": noise(arg_keys[6], (FF, D), FF ** -0.5, 0.0625, ((0, 4),)),
        "lead_factors": noise(arg_keys[7], (5, ADAPTERS, D, RANK), D ** -0.5, 0.125),
        "head_factors": noise(arg_keys[8], (3, ADAPTERS, RANK, D), (16 * RANK) ** -0.5, 0.375, ((3, 4),)),
        "unit_factors": noise(arg_keys[9], (2, ADAPTERS, RANK, FF), (16 * RANK) ** -0.5, 0.375, ((3, 4),)),
        "merge_factors": noise(arg_keys[10], (ADAPTERS, D, RANK), (D // 8) ** -0.5, 0.375, ((1, 4),)),
        "down_factors": noise(arg_keys[11], (ADAPTERS, FF, RANK), FF ** -0.5, 0.0625, ((1, 4),)),
        "tail_factors": noise(arg_keys[12], (2, ADAPTERS, RANK, D), (16 * RANK) ** -0.5, 0.375),
        "doc_ids": jax.vmap(lambda own: jnp.searchsorted(jnp.cumsum(uneven_parts(own, SEQ_LEN // 8, SEQ_LEN, SEQ_LEN // 2, 2)), jnp.arange(SEQ_LEN), side="right"))(jax.random.split(arg_keys[13], SEQS)).reshape((SEQS, SEQ_LEN)).astype(jnp.int32),
        "keep_mask": set_ends((jax.random.randint(arg_keys[14], (SEQS, SEQ_LEN), 0, 8) < 7).astype(jnp.int32), jax.random.fold_in(arg_keys[14], 1), 0, 1),
        "adapter_pick": picks_of(arg_keys[15], SEQS, ADAPTERS, 1, 0),
    }


EPSILON = 1e-05
ROPE_BASE = 130000.0
ADAPTER_SCALING = 2.0
MASKED = -1000000000.0
EXACT_PRECISION = lax.Precision.HIGHEST

@jax.custom_vjp
def low(v):
    return lax.optimization_barrier(v.astype(jnp.bfloat16)).astype(jnp.float32)

@jax.custom_vjp
def reduced_backward(v):
    return v

def low_keep(v):
    return (low(v), None)

def low_pass(kept, grad):
    return (grad,)

def back_keep(v):
    return (v, None)

def back_low(kept, grad):
    return (low(grad),)
low.defvjp(low_keep, low_pass)
reduced_backward.defvjp(back_keep, back_low)

def tables(length):
    half_width = HEAD_DIM // 2
    frequency = ROPE_BASE ** (-jnp.arange(half_width, dtype=jnp.float32) * (2.0 / HEAD_DIM))
    angles = jnp.arange(length, dtype=jnp.float32)[:, None] * frequency[None, :]
    return (jnp.cos(angles)[:, None, :], jnp.sin(angles)[:, None, :])

def rotate(value_rows, cosine_table, sine_table):
    half_width = value_rows.shape[-1] // 2
    first_half = value_rows[..., :half_width]
    second_half = value_rows[..., half_width:]
    return jnp.concatenate([first_half * cosine_table - second_half * sine_table, second_half * cosine_table + first_half * sine_table], axis=-1)

def permit(segments, kept_keys, first_row, last_row):
    rows_at = jnp.arange(first_row, last_row)[:, None]
    keys_at = jnp.arange(last_row)[None, :]
    same_doc = segments[first_row:last_row][:, None] == segments[:last_row][None, :]
    live_key = (kept_keys[:last_row][None, :] == 1) | (rows_at == keys_at)
    return (keys_at <= rows_at) & same_doc & live_key

def rms_norm(stream, norm_gain):
    return stream * lax.rsqrt(lax.optimization_barrier(jnp.mean(stream * stream, axis=-1, keepdims=True)) + EPSILON) * norm_gain

def adapter_distribute(normalized, first_factor, second_factor):
    low_mid = low(jnp.dot(normalized, first_factor, precision=EXACT_PRECISION))
    group_mids = reduced_backward(jnp.broadcast_to(low_mid[None], (N_TENSOR,) + low_mid.shape))
    group_width = second_factor.shape[1] // N_TENSOR
    pieces = jnp.einsum('gtr,rgw->tgw', group_mids, second_factor.reshape(second_factor.shape[0], N_TENSOR, group_width), precision=EXACT_PRECISION)
    return pieces.reshape(normalized.shape[0], second_factor.shape[1])

def adapter_collect(value_rows, first_factor, second_factor):
    group_width = value_rows.shape[1] // N_TENSOR
    group_mids = jnp.einsum('tgw,gwr->gtr', value_rows.reshape(value_rows.shape[0], N_TENSOR, group_width), first_factor.reshape(N_TENSOR, group_width, first_factor.shape[1]), precision=EXACT_PRECISION)
    group_mids = reduced_backward(low(group_mids))
    return jnp.einsum('gtr,rd->td', group_mids, second_factor, precision=EXACT_PRECISION)

def forward_layer(stream, adapters, frozen, allowed, cosine_table, sine_table, chosen):
    norm_gains, query_key_value_matrix, output_matrix, gate_up_matrix, down_matrix = frozen
    lead_all, head_all, unit_all, merge_all, down_all, tail_all = adapters
    leading_selection = lax.dynamic_index_in_dim(lead_all, chosen, 1, keepdims=False)
    head_selection = lax.dynamic_index_in_dim(head_all, chosen, 1, keepdims=False)
    unit_selection = lax.dynamic_index_in_dim(unit_all, chosen, 1, keepdims=False)
    merged_selection = lax.dynamic_index_in_dim(merge_all, chosen, 0, keepdims=False)
    shrinking_selection = lax.dynamic_index_in_dim(down_all, chosen, 0, keepdims=False)
    trailing_selection = lax.dynamic_index_in_dim(tail_all, chosen, 1, keepdims=False)
    length = stream.shape[0]
    first_normalized = low(rms_norm(stream, norm_gains[0]))
    projection_result = [jnp.dot(first_normalized, query_key_value_matrix[0], precision=EXACT_PRECISION) + ADAPTER_SCALING * adapter_distribute(first_normalized, leading_selection[0], head_selection[0]), jnp.dot(first_normalized, query_key_value_matrix[1], precision=EXACT_PRECISION) + ADAPTER_SCALING * adapter_distribute(first_normalized, leading_selection[1], head_selection[1]), jnp.dot(first_normalized, query_key_value_matrix[2], precision=EXACT_PRECISION) + ADAPTER_SCALING * adapter_distribute(first_normalized, leading_selection[2], head_selection[2])]
    query_rot = low(rotate(reduced_backward(projection_result[0]).reshape(length, HEADS, HEAD_DIM), cosine_table, sine_table))
    key_rot = low(rotate(reduced_backward(projection_result[1]).reshape(length, HEADS, HEAD_DIM), cosine_table, sine_table))
    valued = low(reduced_backward(projection_result[2])).reshape(length, HEADS, HEAD_DIM)
    scores = reduced_backward(jnp.einsum('qhe,khe->hqk', query_rot, key_rot, precision=EXACT_PRECISION) * (1.0 / math.sqrt(HEAD_DIM)))
    scores = jnp.where(allowed[None], scores, MASKED)
    weights = low(jax.nn.softmax(scores, axis=-1))
    attention_result = jnp.einsum('hqk,khe->qhe', weights, valued, precision=EXACT_PRECISION).reshape(length, D)
    attention_result = low(reduced_backward(attention_result))
    adapter_branch = jnp.dot(attention_result, output_matrix, precision=EXACT_PRECISION) + ADAPTER_SCALING * adapter_collect(attention_result, merged_selection, trailing_selection[0])
    first_hidden = stream + reduced_backward(adapter_branch)
    second_normalized = low(rms_norm(first_hidden, norm_gains[1]))
    gate_activation = reduced_backward(jnp.dot(second_normalized, gate_up_matrix[0], precision=EXACT_PRECISION) + ADAPTER_SCALING * adapter_distribute(second_normalized, leading_selection[3], unit_selection[0]))
    up_activation = reduced_backward(jnp.dot(second_normalized, gate_up_matrix[1], precision=EXACT_PRECISION) + ADAPTER_SCALING * adapter_distribute(second_normalized, leading_selection[4], unit_selection[1]))
    hidden_state = low(jax.nn.silu(gate_activation) * up_activation)
    return first_hidden + jnp.dot(hidden_state, down_matrix, precision=EXACT_PRECISION) + ADAPTER_SCALING * adapter_collect(hidden_state, shrinking_selection, trailing_selection[1])

def reference(tokens, cotangent, norm_gains, query_key_value_matrix, output_matrix, gate_up_matrix, down_matrix, lead_factors, head_factors, unit_factors, merge_factors, down_factors, tail_factors, doc_ids, keep_mask, adapter_pick):
    frozen = tuple((weight.astype(jnp.float32) for weight in (norm_gains, query_key_value_matrix, output_matrix, gate_up_matrix, down_matrix)))
    factors = tuple((factor.astype(jnp.float32) for factor in (lead_factors, head_factors, unit_factors, merge_factors, down_factors, tail_factors)))
    cosine_table, sine_table = tables(SEQ_LEN)

    def sequence_step(running, inputs_now):
        seq_rows, upstream, segments, kept_keys, chosen = inputs_now
        allowed = permit(segments, kept_keys, 0, SEQ_LEN)

        def layer_of(stream, lead_all, head_all, unit_all, merge_all, down_all, tail_all):
            return forward_layer(stream, (lead_all, head_all, unit_all, merge_all, down_all, tail_all), frozen, allowed, cosine_table, sine_table, chosen)
        layer_out, pullback = jax.vjp(layer_of, seq_rows.astype(jnp.float32), factors[0], factors[1], factors[2], factors[3], factors[4], factors[5])
        gradients = pullback(upstream.astype(jnp.float32))
        running = tuple((running_sum + gradient for running_sum, gradient in zip(running, gradients[1:])))
        return (running, (layer_out.astype(jnp.bfloat16), gradients[0].astype(jnp.bfloat16)))
    initial = tuple((jnp.zeros(factor.shape, jnp.float32) for factor in factors))
    factor_sums, outputs = lax.scan(sequence_step, initial, (tokens, cotangent, doc_ids, keep_mask, adapter_pick[:, 0]))
    return (outputs[0], outputs[1], factor_sums[0], factor_sums[1], factor_sums[2], factor_sums[3], factor_sums[4], factor_sums[5])
```

```python
import functools
import math

import jax
import jax.numpy as jnp
from jax import lax
from jax.experimental import pallas as pl
from jax.experimental.pallas import tpu as pltpu
from jax.sharding import PartitionSpec as P

HEAD_DIM = 64
EPSILON = 1e-05
ROPE_BASE = 130000.0
SCALING = 2.0
MASKED = -1000000000.0
LONGEST_DOC = 512
CHUNKS = 2
MODES = {
    "tok": ("stack", "stack"),
    "cot": ("pair", "pair"),
    "branch": ("stack", "pair"),
    "hidden": ("stack", "stack"),
    "feed": ("pair", "pair"),
    "back": ("stack", "pair"),
    "grad": ("stack", "stack"),
    "last": ("pair", "stack"),
}
SUB_ROWS = 256
VMEM_LIMIT = 60 * 1024 * 1024

BESIDE = [(0, 1), (1, 0), (2, 3), (3, 2)]
MIDDLE = [(1, 2), (2, 1)]
OVER = [(0, 2), (3, 1)]
ACROSS = [(1, 3), (2, 0)]
OUTWARD = [(1, 0), (2, 3)]
INWARD = [(0, 1), (3, 2)]

F32 = jnp.float32
BF16 = jnp.bfloat16


def dot(a, b):
    return jnp.dot(a, b, preferred_element_type=F32)


def dot_nt(a, b):
    return lax.dot_general(a, b, (((1,), (1,)), ((), ())), preferred_element_type=F32)


def dot_tn(a, b):
    return lax.dot_general(a, b, (((0,), (0,)), ((), ())), preferred_element_type=F32)


def whole(array):
    rank = len(array.shape)
    return pl.BlockSpec(array.shape, lambda *_: (0,) * rank, pipeline_mode=pl.Buffered(1))


ANY = pl.BlockSpec(memory_space=pl.ANY)


def out_whole(shape):
    rank = len(shape)
    return pl.BlockSpec(shape, lambda *_: (0,) * rank)


def spread(own, mode):
    if mode == "stack":
        return [lax.all_gather(own, "tensor", axis=0, tiled=False)]
    beside = lax.ppermute(own, "tensor", BESIDE)
    near = lax.ppermute(own, "tensor", MIDDLE)
    far = lax.ppermute(own, "tensor", OVER)
    return [
        own,
        beside,
        near,
        far,
        lax.ppermute(near, "tensor", OUTWARD),
        lax.ppermute(far, "tensor", OUTWARD),
    ]


def slab_columns(slab, width):
    return pl.ds(pl.multiple_of(slab * width, width), width)


def slab_copies(state, parts, target, sems):
    width = parts[0].shape[-1]
    if len(parts) == 1:
        return [
            (None, pltpu.make_async_copy(
                parts[0].at[j], target.at[:, j * width : (j + 1) * width], sems.at[j]
            ))
            for j in range(parts[0].shape[0])
        ]
    me, inner, near, far = places(state)
    copies = []
    for sem, (condition, part, slab) in enumerate((
        (None, parts[0], me),
        (None, parts[1], beside_of(me)),
        (inner, parts[2], near),
        (inner, parts[3], far),
        (jnp.logical_not(inner), parts[4], near),
        (jnp.logical_not(inner), parts[5], far),
    )):
        copies.append((condition, pltpu.make_async_copy(
            part, target.at[:, slab_columns(slab, width)], sems.at[sem % 4 + 2 * (sem // 4)]
        )))
    return copies


def beside_of(me):
    return me + 1 - 2 * lax.rem(me, 2)


def places(state):
    me = state[0]
    upper = me >= 2
    return me, (me == 1) | (me == 2), jnp.where(upper, 1, 2), jnp.where(upper, 0, 3)


def each_copy(copies, act):
    for condition, copy in copies:
        if condition is None:
            act(copy)
        else:
            pl.when(condition)(functools.partial(act, copy))


def start_copies(copies):
    each_copy(copies, lambda copy: copy.start())


def wait_copies(copies):
    each_copy(copies, lambda copy: copy.wait())


def write_slabs(state, outs, term):
    width = outs[0].shape[-1]
    if len(outs) == 1:
        for slab in range(outs[0].shape[0]):
            outs[0][slab] = term(slab_columns(slab, width)).astype(BF16)
        return
    me, _, near, far = places(state)
    for target, slab in (
        (outs[0].at[0], near),
        (outs[0].at[1], far),
        (outs[1], beside_of(me)),
        (outs[2], me),
    ):
        target[...] = term(slab_columns(slab, width)).astype(BF16)


def slab_outs(mode, count, rows, width):
    if mode == "stack":
        shapes = ((count, rows, width),)
    else:
        shapes = ((2, rows, width), (rows, width), (rows, width))
    return (
        tuple(jax.ShapeDtypeStruct(shape, BF16) for shape in shapes),
        tuple(out_whole(shape) for shape in shapes),
    )


def add_kernel(state, far, received, beside, near_out, far_out, beside_out):
    near_out[...] = (far[0].astype(F32) + received[0].astype(F32)).astype(BF16)
    far_out[...] = (far[1].astype(F32) + received[1].astype(F32)).astype(BF16)
    beside_out[...] = beside[...]


def sum_kernel(state, *refs):
    terms, (exact, rounded) = refs[:-2], refs[-2:]
    total = terms[0][...].astype(F32)
    for term in terms[1:]:
        total += term[...].astype(F32)
    exact[...] = total
    rounded[...] = total.astype(BF16)


def sum_after_kernel(count, state, first, *refs):
    terms, joined = refs[:-1], refs[-1]
    step = pl.program_id(0)

    @pl.when(step < count)
    def _():
        joined[...] = first[...]

    @pl.when(step >= count)
    def _():
        total = terms[0][...].astype(F32)
        for term in terms[1:]:
            total += term[...].astype(F32)
        joined[...] = total.astype(BF16)


def relay_kernel(state, *refs):
    count = len(refs) // 2
    for source, target in zip(refs[:count], refs[count:]):
        target[...] = source[...]


def relay(line, parts):
    return line.call(
        relay_kernel,
        "relay",
        (1,),
        parts,
        [whole(x) for x in parts],
        tuple(jax.ShapeDtypeStruct(x.shape, x.dtype) for x in parts),
        tuple(out_whole(x.shape) for x in parts),
    )


class SlabSum:
    def __init__(self, line, parts):
        self.line, self.parts = line, parts
        if len(parts) == 1:
            self.terms = [
                lax.psum_scatter(parts[0], "tensor", scatter_dimension=0, tiled=False)
            ]
        else:
            self.received = lax.ppermute(parts[0], "tensor", INWARD)

    def cross(self, after=()):
        far, beside, own = self.parts
        rows, width = own.shape
        step = min(256, rows)
        flat = pl.BlockSpec((step, width), lambda i, s: (i, 0))
        both = pl.BlockSpec((2, step, width), lambda i, s: (0, i, 0))
        near, far, beside = self.line.call(
            add_kernel,
            "add",
            (rows // step,),
            (far, self.received, beside),
            [both, both, flat],
            (jax.ShapeDtypeStruct((rows, width), BF16),) * 3,
            (flat,) * 3,
            after=after,
        )
        near = lax.ppermute(near, "tensor", MIDDLE)
        far = lax.ppermute(far, "tensor", ACROSS)
        beside = lax.ppermute(beside, "tensor", BESIDE)
        self.terms = [own, beside, near, far]

    def finish(self, base, after=()):
        rows, width = base.shape
        step = min(256, rows)
        flat = pl.BlockSpec((step, width), lambda i, s: (i, 0))
        return self.line.call(
            sum_kernel,
            "sum",
            (rows // step,),
            (base, *self.terms),
            [flat] * (1 + len(self.terms)),
            (jax.ShapeDtypeStruct((rows, width), F32), jax.ShapeDtypeStruct((rows, width), BF16)),
            (flat, flat),
            after=after,
        )


    def finish_after(self, base, first):
        rows, width = base.shape
        step = min(256, rows)
        count = rows // step
        flat = pl.BlockSpec((step, width), lambda i, s: (jnp.maximum(i - count, 0), 0))
        return self.line.call(
            functools.partial(sum_after_kernel, count),
            "sum_after",
            (2 * count,),
            (first, base, *self.terms),
            [pl.BlockSpec((step, width), lambda i, s: (jnp.minimum(i, count - 1), 0))]
            + [flat] * (1 + len(self.terms)),
            jax.ShapeDtypeStruct((2 * rows, width), BF16),
            pl.BlockSpec((step, width), lambda i, s: (i, 0)),
        )


def params(grid_rank=1):
    return pltpu.CompilerParams(
        dimension_semantics=("arbitrary",) * grid_rank, vmem_limit_bytes=VMEM_LIMIT
    )


class Line:
    def __init__(self, state):
        self.state, self.last = state, ()

    def call(self, kernel, name, grid, ins, in_specs, outs, out_specs, scratch=(), after=()):
        after = (*self.last, *after)
        n_used = 1 + len(ins)

        def body(*refs):
            kernel(*refs[:n_used], *refs[n_used + len(after) :])

        results = pl.pallas_call(
            body,
            name=name,
            grid_spec=pltpu.PrefetchScalarGridSpec(
                num_scalar_prefetch=1,
                grid=grid,
                in_specs=list(in_specs) + [ANY] * len(after),
                out_specs=out_specs,
                scratch_shapes=list(scratch),
            ),
            out_shape=outs,
            compiler_params=params(len(grid)),
            cost_estimate=pl.CostEstimate(flops=1, bytes_accessed=1, transcendentals=0),
        )(self.state, *ins, *after)
        self.last = (jax.tree.leaves(results)[-1],)
        return results


def swap_halves(values):
    width = values.shape[-1]
    half = HEAD_DIM // 2
    lane = lax.broadcasted_iota(jnp.int32, values.shape, values.ndim - 1) % HEAD_DIM
    return jnp.where(
        lane < half,
        pltpu.roll(values, width - half, values.ndim - 1),
        pltpu.roll(values, half, values.ndim - 1),
    )


def rope_groups(values, cosine, sine, sign):
    groups = []
    for first in range(0, values.shape[-1], 128):
        group = values[:, first : first + 128]
        groups.append(group * cosine + (sign * swap_halves(group)) * sine)
    return jnp.concatenate(groups, axis=-1)


def project_kernel(n_parts, state, *refs):
    parts, refs = refs[:n_parts], refs[n_parts:]
    gain, lead, weight, head, cosine, sine, qkv, normed, mid, scale, stream, sems = refs
    step = pl.program_id(0)
    rank = lead.shape[2]

    @pl.when(step == 0)
    def _():
        copies = slab_copies(state, parts, stream, sems)
        start_copies(copies)
        wait_copies(copies)
        for first in range(0, stream.shape[0], SUB_ROWS):
            here = pl.ds(first, SUB_ROWS)
            rows = stream[here, :].astype(F32)
            r1 = lax.rsqrt(jnp.mean(rows * rows, axis=1, keepdims=True) + EPSILON)
            scale[here, :] = r1
            values = (rows * r1 * gain[0:1, :]).astype(BF16)
            normed[here, :] = values
            mids = dot_nt(values, lead[:3, 0].reshape(3 * rank, -1))
            for j in range(3):
                mid[j, here, :] = mids[:, j * rank : (j + 1) * rank].astype(BF16)

    for first in range(0, stream.shape[0], SUB_ROWS):
        here = pl.ds(first, SUB_ROWS)
        projected = dot(normed[here, :], weight[0]) + SCALING * dot(mid[step, here, :], head[0, 0])

        @pl.when(step < 2)
        def _():
            qkv[0, here, :] = rope_groups(projected, cosine[here, :], sine[here, :], 1.0).astype(BF16)

        @pl.when(step == 2)
        def _():
            qkv[0, here, :] = projected.astype(BF16)


def project(line, parts, gains, lead, weight, head, cosine, sine, after=()):
    rows = parts[0].shape[-2]
    full, width = weight.shape[1:]
    rank = lead.shape[2]
    slabs = full // parts[0].shape[-1]
    return line.call(
        functools.partial(project_kernel, len(parts)),
        "project",
        (3,),
        (*parts, gains, lead, weight, head, cosine, sine),
        [ANY] * len(parts)
        + [
            whole(gains),
            pl.BlockSpec(
                (lead.shape[0], 1, rank, full),
                lambda j, s: (0, s[1], 0, 0),
                pipeline_mode=pl.Buffered(1),
            ),
            pl.BlockSpec((1, full, width), lambda j, s: (j, 0, 0)),
            pl.BlockSpec((1, 1, rank, width), lambda j, s: (j, s[1], 0, 0)),
            whole(cosine),
            whole(sine),
        ],
        (
            jax.ShapeDtypeStruct((3, rows, width), BF16),
            jax.ShapeDtypeStruct((rows, full), BF16),
            jax.ShapeDtypeStruct((3, rows, rank), BF16),
            jax.ShapeDtypeStruct((rows, 1), F32),
        ),
        (
            pl.BlockSpec((1, rows, width), lambda j, s: (j, 0, 0)),
            out_whole((rows, full)),
            out_whole((3, rows, rank)),
            out_whole((rows, 1)),
        ),
        [pltpu.VMEM((rows, full), BF16), pltpu.SemaphoreType.DMA((slabs,))],
        after,
    )


def head_mask(shape, half):
    lane = lax.broadcasted_iota(jnp.int32, shape, len(shape) - 1)
    return (lane >= HEAD_DIM) if half else (lane < HEAD_DIM)


def key_span(first_row, block):
    low = max(0, first_row - LONGEST_DOC + 1)
    return (low // 128) * 128, first_row + block


def key_bias(doc_rows, doc_keys, keep_keys, first_row, low, high, block):
    rows_at = first_row + lax.broadcasted_iota(jnp.int32, (block, high - low), 0)
    keys_at = low + lax.broadcasted_iota(jnp.int32, (block, high - low), 1)
    same = doc_rows == doc_keys[:, low:high]
    live = (keep_keys[:, low:high] == 1) | (rows_at == keys_at)
    return jnp.where((keys_at <= rows_at) & same & live, 0.0, MASKED)


def attend_kernel(first_row, block, n_chunks, n_outs, state, *refs):
    chunks, refs = refs[: 2 * n_chunks], refs[2 * n_chunks :]
    query, doc_rows, doc_keys, keep, weight, merge, tail = refs[:7]
    attended, refs = refs[7], refs[8:]
    branch, (keys, values, bias, held) = refs[:n_outs], refs[n_outs:]
    step = pl.program_id(0)
    rows = query.shape[1]
    for c in range(n_chunks):
        keys[c * rows : (c + 1) * rows, :] = chunks[2 * c][0]
        values[c * rows : (c + 1) * rows, :] = chunks[2 * c + 1][0]
    for sub in range(rows // block):
        start = first_row + sub * block
        low, high = key_span(start, block)
        here = pl.ds(sub * block, block)

        @pl.when(step == 0)
        def _():
            bias[sub, :, : high - low] = key_bias(
                doc_rows[here, :], doc_keys[...], keep[...], start, low, high, block
            )

        outs = []
        for half in range(2):
            mask = head_mask((block, 128), half)
            q = jnp.where(mask, query[0, here, :] * (HEAD_DIM**-0.5), 0.0).astype(BF16)
            scores = dot_nt(q, keys[low:high, :]) + bias[sub, :, : high - low]
            raised = jnp.exp(scores - jnp.max(scores, axis=1, keepdims=True))
            total = jnp.sum(raised, axis=1, keepdims=True)
            weights = (raised * (1.0 / total)).astype(BF16)
            outs.append(dot(weights, values[low:high, :]))
        columns = pl.ds(pl.multiple_of(step * 128, 128), 128)
        held[here, columns] = jnp.where(head_mask((block, 128), 0), outs[0], outs[1]).astype(BF16)

    @pl.when(step == pl.num_programs(0) - 1)
    def _():
        result = held[...]
        attended[...] = result
        mid = dot_nt(result, merge[0]).astype(BF16)
        write_slabs(
            state,
            branch,
            lambda columns: dot(result, weight[:, columns])
            + SCALING * dot(mid, tail[0, 0, :, columns]),
        )


def attend(line, qkvs, chunk, doc_column, doc_row, keep_row, weight, merge, tail, slabs, mode, after=()):
    rows, width = qkvs[0].shape[1:]
    first_row = chunk * rows
    block = min(256, rows)
    n_chunks = chunk + 1
    rank, full = merge.shape[1], weight.shape[1]
    ins, specs = [], []
    for c in range(n_chunks):
        for j in (1, 2):
            ins.append(qkvs[c])
            specs.append(pl.BlockSpec((1, rows, 128), lambda i, s, j=j: (j, 0, i)))
    ins += [qkvs[chunk], doc_column, doc_row, keep_row, weight, merge, tail]
    specs += [
        pl.BlockSpec((1, rows, 128), lambda i, s: (0, 0, i)),
        pl.BlockSpec((rows, 1), lambda i, s: (chunk, 0), pipeline_mode=pl.Buffered(1)),
        whole(doc_row),
        whole(keep_row),
        whole(weight),
        pl.BlockSpec((1, rank, width), lambda i, s: (s[1], 0, 0), pipeline_mode=pl.Buffered(1)),
        pl.BlockSpec(
            (1, 1, rank, full), lambda i, s: (0, s[1], 0, 0), pipeline_mode=pl.Buffered(1)
        ),
    ]
    n_keys = first_row + rows
    shapes, out_specs = slab_outs(mode, slabs, rows, full // slabs)
    outs = line.call(
        functools.partial(attend_kernel, first_row, block, n_chunks, len(shapes)),
        "attend",
        (width // 128,),
        ins,
        specs,
        (jax.ShapeDtypeStruct((rows, width), BF16),) + shapes,
        (out_whole((rows, width)),) + out_specs,
        [
            pltpu.VMEM((n_keys, 128), BF16),
            pltpu.VMEM((n_keys, 128), BF16),
            pltpu.VMEM((rows // block, block, min(n_keys, LONGEST_DOC + block)), F32),
            pltpu.VMEM((rows, width), BF16),
        ],
        after,
    )
    return outs


def feed_kernel(n_parts, n_cots, n_feed, n_back, state, *refs):
    parts, refs = refs[:n_parts], refs[n_parts:]
    cot_parts, refs = refs[:n_cots], refs[n_cots:]
    gain, lead, gate_w, up_w, down_w, unit, down, tail = refs[:8]
    refs = refs[8:]
    feed, refs = refs[:n_feed], refs[n_feed:]
    back, refs = refs[:n_back], refs[n_back:]
    unit_grad, down_grad, lead_grad, tail_grad = refs[:4]
    stream, upstream, normed, mid, down_back, scale = refs[4:10]
    feed_sum, back_sum, down_mid, unit_back, sems, cot_sems = refs[10:]
    step = pl.program_id(0)
    rank = lead.shape[2]
    firsts = range(0, stream.shape[0], SUB_ROWS)

    @pl.when(step == 0)
    def _():
        copies = slab_copies(state, parts, stream, sems)
        cot_copies = slab_copies(state, cot_parts, upstream, cot_sems)
        start_copies(copies)
        start_copies(cot_copies)
        wait_copies(copies)
        for first in firsts:
            here = pl.ds(first, SUB_ROWS)
            rows = stream[here, :].astype(F32)
            r2 = lax.rsqrt(jnp.mean(rows * rows, axis=1, keepdims=True) + EPSILON)
            scale[here, :] = r2
            values = (rows * r2 * gain[1:2, :]).astype(BF16)
            normed[here, :] = values
            mids = dot_nt(values, lead[3:5, 0].reshape(2 * rank, -1))
            for j in range(2):
                mid[j, here, :] = mids[:, j * rank : (j + 1) * rank].astype(BF16)
        wait_copies(cot_copies)
        down_back[...] = (SCALING * dot_nt(upstream[...], tail[0, 0])).astype(BF16)
        feed_sum[...] = jnp.zeros_like(feed_sum)
        back_sum[...] = jnp.zeros_like(back_sum)
        down_mid[...] = jnp.zeros_like(down_mid)
        unit_back[...] = jnp.zeros_like(unit_back)

    unit_terms = [0.0, 0.0]
    down_term = 0.0
    for first in firsts:
        here = pl.ds(first, SUB_ROWS)
        gate = dot(normed[here, :], gate_w[0]) + SCALING * dot(mid[0, here, :], unit[0, 0])
        up = dot(normed[here, :], up_w[0]) + SCALING * dot(mid[1, here, :], unit[1, 0])
        hidden_grad = dot_nt(upstream[here, :], down_w[...]) + dot(down_back[here, :], down[0])
        sigma = 1.0 / (1.0 + jnp.exp(-gate))
        active = gate * sigma
        hidden = (active * up).astype(BF16)
        up_grad = (hidden_grad * active).astype(BF16)
        gate_grad = (hidden_grad * up * (sigma + active * (1.0 - sigma))).astype(BF16)
        feed_sum[here, :] += dot(hidden, down_w[...])
        back_sum[here, :] += dot_nt(gate_grad, gate_w[0]) + dot_nt(up_grad, up_w[0])
        down_mid[here, :] += dot_nt(hidden, down[0])
        unit_back[0, here, :] += dot_nt(gate_grad, unit[0, 0])
        unit_back[1, here, :] += dot_nt(up_grad, unit[1, 0])
        unit_terms[0] += dot_tn(mid[0, here, :], gate_grad)
        unit_terms[1] += dot_tn(mid[1, here, :], up_grad)
        down_term += dot_tn(down_back[here, :], hidden)
    unit_grad[0] = SCALING * unit_terms[0]
    unit_grad[1] = SCALING * unit_terms[1]
    down_grad[...] = down_term

    @pl.when(step == pl.num_programs(0) - 1)
    def _():
        values = normed[...]
        mid_down = down_mid[...].astype(BF16)
        tail_grad[...] = SCALING * dot_tn(mid_down, upstream[...])
        unit_backs = [(SCALING * unit_back[j]).astype(BF16) for j in range(2)]
        for j in range(2):
            lead_grad[j] = dot_tn(unit_backs[j], values)
        write_slabs(
            state,
            feed,
            lambda columns: feed_sum[:, columns] + SCALING * dot(mid_down, tail[0, 0, :, columns]),
        )
        for first in firsts:
            here = pl.ds(first, SUB_ROWS)
            there = slice(first, first + SUB_ROWS)
            r2 = scale[here, :]
            total = back_sum[here, :]
            for j in range(2):
                total += dot(unit_backs[j][there], lead[3 + j, 0])
            inner = jnp.mean(total * normed[here, :].astype(F32), axis=1, keepdims=True)
            back_sum[here, :] = r2 * (
                gain[1:2, :] * total - stream[here, :].astype(F32) * (r2 * inner)
            )
        write_slabs(state, back, lambda columns: back_sum[:, columns])


def feed_forward(
    line, parts, cot_parts, gains, lead, gate_up, down_w, unit, down, tail, modes, after=()
):
    feed_mode, back_mode = modes
    rows, slab_width = parts[0].shape[-2:]
    full, units = gate_up.shape[1:]
    rank = lead.shape[2]
    slabs = full // slab_width
    block = min(512, units)
    feed_shapes, feed_specs = slab_outs(feed_mode, slabs, rows, slab_width)
    back_shapes, back_specs = slab_outs(back_mode, slabs, rows, slab_width)
    outs = line.call(
        functools.partial(
            feed_kernel, len(parts), len(cot_parts), len(feed_shapes), len(back_shapes)
        ),
        "feed_forward",
        (units // block,),
        (*parts, *cot_parts, gains, lead, gate_up, gate_up, down_w, unit, down, tail),
        [ANY] * (len(parts) + len(cot_parts))
        + [
            whole(gains),
            pl.BlockSpec(
                (lead.shape[0], 1, rank, full),
                lambda i, s: (0, s[1], 0, 0),
                pipeline_mode=pl.Buffered(1),
            ),
            pl.BlockSpec((1, full, block), lambda i, s: (0, 0, i)),
            pl.BlockSpec((1, full, block), lambda i, s: (1, 0, i)),
            pl.BlockSpec((block, full), lambda i, s: (i, 0)),
            pl.BlockSpec((2, 1, rank, block), lambda i, s: (0, s[1], 0, i)),
            pl.BlockSpec((1, rank, block), lambda i, s: (s[1], 0, i)),
            pl.BlockSpec(
                (1, 1, rank, full), lambda i, s: (1, s[1], 0, 0), pipeline_mode=pl.Buffered(1)
            ),
        ],
        feed_shapes
        + back_shapes
        + (
            jax.ShapeDtypeStruct((2, rank, units), F32),
            jax.ShapeDtypeStruct((rank, units), F32),
            jax.ShapeDtypeStruct((2, rank, full), F32),
            jax.ShapeDtypeStruct((rank, full), F32),
        ),
        feed_specs
        + back_specs
        + (
            pl.BlockSpec((2, rank, block), lambda i, s: (0, 0, i)),
            pl.BlockSpec((rank, block), lambda i, s: (0, i)),
            out_whole((2, rank, full)),
            out_whole((rank, full)),
        ),
        [
            pltpu.VMEM((rows, full), BF16),
            pltpu.VMEM((rows, full), BF16),
            pltpu.VMEM((rows, full), BF16),
            pltpu.VMEM((2, rows, rank), BF16),
            pltpu.VMEM((rows, rank), BF16),
            pltpu.VMEM((rows, 1), F32),
            pltpu.VMEM((rows, full), F32),
            pltpu.VMEM((rows, full), F32),
            pltpu.VMEM((rows, rank), F32),
            pltpu.VMEM((2, rows, rank), F32),
            pltpu.SemaphoreType.DMA((slabs,)),
            pltpu.SemaphoreType.DMA((slabs,)),
        ],
        after,
    )
    n_feed, n_both = len(feed_shapes), len(feed_shapes) + len(back_shapes)
    return list(outs[:n_feed]), list(outs[n_feed:n_both]), outs[n_both:]


def attend_back_kernel(first_row, block, n_chunks, n_parts, state, *refs):
    parts, refs = refs[:n_parts], refs[n_parts:]
    chunks, refs = refs[: 2 * n_chunks], refs[2 * n_chunks :]
    query, doc_rows, doc_keys, keep, attended, weight, merge, tail = refs[:8]
    query_grad, key_grad, value_grad, merge_grad, tail_grad = refs[8:13]
    keys, values, bias, branch, out_grad, sems = refs[13:]
    step = pl.program_id(0)
    rows = query.shape[1]
    inverse_root = HEAD_DIM**-0.5

    @pl.when(step == 0)
    def _():
        copies = slab_copies(state, parts, branch, sems)
        start_copies(copies)
        wait_copies(copies)
        gradient = branch[...]
        result = attended[...]
        merge_back = (SCALING * dot_nt(gradient, tail[0, 0])).astype(BF16)
        merge_mid = dot_nt(result, merge[0]).astype(BF16)
        merge_grad[...] = dot_tn(merge_back, result)
        tail_grad[...] = SCALING * dot_tn(merge_mid, gradient)
        whole_grad = (dot_nt(gradient, weight[...]) + dot(merge_back, merge[0])).astype(BF16)
        for pair in range(out_grad.shape[0]):
            out_grad[pair] = whole_grad[:, pair * 128 : (pair + 1) * 128]

    for c in range(n_chunks):
        keys[c * rows : (c + 1) * rows, :] = chunks[2 * c][0]
        values[c * rows : (c + 1) * rows, :] = chunks[2 * c + 1][0]
    key_grad[...] = jnp.zeros_like(key_grad)
    value_grad[...] = jnp.zeros_like(value_grad)
    for sub in range(rows // block):
        start = first_row + sub * block
        low, high = key_span(start, block)
        here = pl.ds(sub * block, block)

        @pl.when(step == 0)
        def _():
            bias[sub, :, : high - low] = key_bias(
                doc_rows[here, :], doc_keys[...], keep[...], start, low, high, block
            )

        outs = []
        key_term = value_term = 0.0
        for half in range(2):
            mask = head_mask((block, 128), half)
            q = jnp.where(mask, query[0, here, :] * inverse_root, 0.0).astype(BF16)
            grad = jnp.where(mask, out_grad[step, here, :], 0.0).astype(BF16)
            scores = dot_nt(q, keys[low:high, :]) + bias[sub, :, : high - low]
            raised = jnp.exp(scores - jnp.max(scores, axis=1, keepdims=True))
            probs = raised * (1.0 / jnp.sum(raised, axis=1, keepdims=True))
            prob_grad = dot_nt(grad, values[low:high, :])
            inner = jnp.sum(probs * prob_grad, axis=1, keepdims=True)
            score_grad = (probs * (prob_grad - inner)).astype(BF16)
            outs.append(dot(score_grad, keys[low:high, :]))
            key_term += dot_tn(score_grad, q)
            value_term += dot_tn(probs.astype(BF16), grad)
        mixed = jnp.where(head_mask((block, 128), 0), outs[0], outs[1])
        query_grad[here, :] = mixed * inverse_root
        key_grad[low:high, :] += key_term
        value_grad[low:high, :] += value_term


def attend_back(line, parts, qkvs, chunk, doc_column, doc_row, keep_row, attended, weight, merge, tail, after=()):
    rows, width = qkvs[0].shape[1:]
    first_row = chunk * rows
    block = min(256, rows)
    n_chunks = chunk + 1
    rank, full = merge.shape[1], weight.shape[1]
    slabs = full // parts[0].shape[-1]
    ins, specs = list(parts), [ANY] * len(parts)
    for c in range(n_chunks):
        for j in (1, 2):
            ins.append(qkvs[c])
            specs.append(pl.BlockSpec((1, rows, 128), lambda i, s, j=j: (j, 0, i)))
    ins += [qkvs[chunk], doc_column, doc_row, keep_row, attended, weight, merge, tail]
    specs += [
        pl.BlockSpec((1, rows, 128), lambda i, s: (0, 0, i)),
        pl.BlockSpec((rows, 1), lambda i, s: (chunk, 0), pipeline_mode=pl.Buffered(1)),
        whole(doc_row),
        whole(keep_row),
        whole(attended),
        whole(weight),
        pl.BlockSpec((1, rank, width), lambda i, s: (s[1], 0, 0), pipeline_mode=pl.Buffered(1)),
        pl.BlockSpec(
            (1, 1, rank, full), lambda i, s: (0, s[1], 0, 0), pipeline_mode=pl.Buffered(1)
        ),
    ]
    n_keys = first_row + rows
    return line.call(
        functools.partial(attend_back_kernel, first_row, block, n_chunks, len(parts)),
        "attend_back",
        (width // 128,),
        ins,
        specs,
        (
            jax.ShapeDtypeStruct((rows, width), F32),
            jax.ShapeDtypeStruct((n_keys, width), F32),
            jax.ShapeDtypeStruct((n_keys, width), F32),
            jax.ShapeDtypeStruct((rank, width), F32),
            jax.ShapeDtypeStruct((rank, full), F32),
        ),
        (
            pl.BlockSpec((rows, 128), lambda i, s: (0, i)),
            pl.BlockSpec((n_keys, 128), lambda i, s: (0, i)),
            pl.BlockSpec((n_keys, 128), lambda i, s: (0, i)),
            out_whole((rank, width)),
            out_whole((rank, full)),
        ),
        [
            pltpu.VMEM((n_keys, 128), BF16),
            pltpu.VMEM((n_keys, 128), BF16),
            pltpu.VMEM((rows // block, block, min(n_keys, LONGEST_DOC + block)), F32),
            pltpu.VMEM((rows, full), BF16),
            pltpu.VMEM((width // 128, rows, 128), BF16),
            pltpu.SemaphoreType.DMA((slabs,)),
        ],
        after,
    )


def project_back_kernel(n_later, n_outs, state, *refs):
    query_grad, refs = refs[0], refs[1:]
    later, refs = refs[: 2 * n_later], refs[2 * n_later :]
    weight, head, lead, gain, normed, mid, scale, cosine, sine = refs[:9]
    outs, refs = refs[9 : 9 + n_outs], refs[9 + n_outs :]
    head_grad, lead_grad, total, held = refs
    step = pl.program_id(0)

    @pl.when(step == 0)
    def _():
        total[...] = jnp.zeros_like(total)
        held[...] = rope_groups(query_grad[...], cosine[...], sine[...], -1.0).astype(BF16)

    def added(which):
        gradient = later[which][...]
        for other in range(1, n_later):
            gradient += later[2 * other + which][...]
        return gradient

    @pl.when(step == 1)
    def _():
        held[...] = rope_groups(added(0), cosine[...], sine[...], -1.0).astype(BF16)

    @pl.when(step == 2)
    def _():
        held[...] = added(1).astype(BF16)

    gradient = held[...]
    values = normed[...]
    back = (SCALING * dot_nt(gradient, head[0, 0])).astype(BF16)
    head_grad[0] = SCALING * dot_tn(mid[0], gradient)
    lead_grad[0] = dot_tn(back, values)
    total[...] += dot_nt(gradient, weight[0]) + dot(back, lead[0, 0])

    @pl.when(step == pl.num_programs(0) - 1)
    def _():
        r1 = scale[...]
        rows = values.astype(F32)
        inner = jnp.mean(total[...] * rows, axis=1, keepdims=True)
        total[...] = r1 * (gain[0:1, :] * total[...] - rows / gain[0:1, :] * inner)
        write_slabs(state, outs, lambda columns: total[:, columns])


def project_back(line, query_grad, later, chunk, weight, head, lead, gains, normed, mid, scale, cosine, sine, slabs, mode, after=()):
    rows, width = query_grad.shape
    full = weight.shape[1]
    rank = lead.shape[2]
    ins, specs = [query_grad], [whole(query_grad)]
    for array in later:
        ins.append(array)
        specs.append(
            pl.BlockSpec((rows, width), lambda j, s: (chunk, 0), pipeline_mode=pl.Buffered(1))
        )
    ins += [weight, head, lead, gains, normed, mid, scale, cosine, sine]
    specs += [
        pl.BlockSpec((1, full, width), lambda j, s: (j, 0, 0)),
        pl.BlockSpec((1, 1, rank, width), lambda j, s: (j, s[1], 0, 0)),
        pl.BlockSpec((1, 1, rank, full), lambda j, s: (j, s[1], 0, 0)),
        whole(gains),
        whole(normed),
        pl.BlockSpec((1, rows, rank), lambda j, s: (j, 0, 0)),
        whole(scale),
        whole(cosine),
        whole(sine),
    ]
    shapes, out_specs = slab_outs(mode, slabs, rows, full // slabs)
    outs = line.call(
        functools.partial(project_back_kernel, len(later) // 2, len(shapes)),
        "project_back",
        (3,),
        ins,
        specs,
        shapes
        + (
            jax.ShapeDtypeStruct((3, rank, width), F32),
            jax.ShapeDtypeStruct((3, rank, full), F32),
        ),
        out_specs
        + (
            pl.BlockSpec((1, rank, width), lambda j, s: (j, 0, 0)),
            pl.BlockSpec((1, rank, full), lambda j, s: (j, 0, 0)),
        ),
        [pltpu.VMEM((rows, full), F32), pltpu.VMEM((rows, width), BF16)],
        after,
    )
    return list(outs[:-2]), outs[-2], outs[-1]


def rope_tables(length):
    half = HEAD_DIM // 2
    frequency = ROPE_BASE ** (-jnp.arange(half, dtype=F32) * (2.0 / HEAD_DIM))
    angles = jnp.arange(length, dtype=F32)[:, None] * frequency[None, :]
    cosine, sine = jnp.cos(angles), jnp.sin(angles)
    return (
        jnp.concatenate([cosine] * 4, axis=1),
        jnp.concatenate([-sine, sine] * 2, axis=1),
    )


def wire_kernel(n_shared, n_pairs, state, *refs):
    pairs, (far, beside, own, split, shared) = refs[: 2 * n_pairs], refs[2 * n_pairs :]
    shared_at = split_at = 0
    for p in range(n_pairs):
        total = (pairs[2 * p][...] + pairs[2 * p + 1][...]).astype(BF16)
        total = total.reshape(-1, total.shape[-1])
        rows = total.shape[0]
        if p < n_shared:
            shared[shared_at : shared_at + rows, :] = total
            shared_at += rows
            continue
        width = split.shape[1]
        for first in range(0, total.shape[1], width):
            split[split_at : split_at + rows, :] = total[:, first : first + width]
            split_at += rows
    write_slabs(state, (far, beside, own), lambda columns: shared[:, columns])
    picked = jnp.full((split.shape[0] - split_at, split.shape[1]), state[1].astype(F32))
    split[split_at:, :] = picked.astype(BF16)


def join_kernel(state, own, beside, near, far, split, joined):
    rows = own.shape[0]
    total = own[...].astype(F32) + beside[...].astype(F32)
    joined[:rows, :] = (total + near[...].astype(F32) + far[...].astype(F32)).astype(BF16)
    joined[rows:, :] = split[...]


def combine_kernel(n_shared, adapters, state, everyone, shared, *split):
    count, rows, width = everyone.shape
    for a in range(adapters):
        total = jnp.zeros((rows - 16, width), F32)
        for d in range(count):
            here = everyone[d, rows - 16 :, :].astype(F32)[:1] == float(a)
            total += jnp.where(here, everyone[d, : rows - 16, :].astype(F32), 0.0)
        shared[a] = total[:n_shared].astype(BF16)
        at = n_shared
        for target in split:
            height, full = target.shape[1:]
            for first in range(0, full, width):
                target[a, :, first : first + width] = total[at : at + height]
                at += height


def whole_width_kernel(state, *refs):
    early, late, (lead, tail) = refs[:6], refs[6:12], refs[12:14]
    early_whole, late_whole, early_sems, late_sems = refs[14:]
    rank, adapters = lead.shape[2], lead.shape[1]
    early_copies = slab_copies(state, early, early_whole, early_sems)
    late_copies = slab_copies(state, late, late_whole, late_sems)
    start_copies(early_copies)
    start_copies(late_copies)
    wait_copies(early_copies)
    wait_copies(late_copies)
    for held, leads, tails in ((late_whole, (0, 1, 2), 0), (early_whole, (3, 4), 1)):
        height = held.shape[0] // adapters
        for a in range(adapters):
            rows = held[a * height : (a + 1) * height, :].astype(F32)
            for i, j in enumerate(leads):
                lead[j, a] = rows[i * rank : (i + 1) * rank]
            tail[tails, a] = rows[len(leads) * rank :]


def whole_width(line, early, late, adapters, rank):
    width = early[0].shape[1]
    full = 4 * width
    return line.call(
        whole_width_kernel,
        "whole_width",
        (1,),
        (*early, *late),
        [ANY] * 12,
        (
            jax.ShapeDtypeStruct((5, adapters, rank, full), F32),
            jax.ShapeDtypeStruct((2, adapters, rank, full), F32),
        ),
        (out_whole((5, adapters, rank, full)), out_whole((2, adapters, rank, full))),
        [
            pltpu.VMEM((early[0].shape[0], full), BF16),
            pltpu.VMEM((late[0].shape[0], full), BF16),
            pltpu.SemaphoreType.DMA((4,)),
            pltpu.SemaphoreType.DMA((4,)),
        ],
    )


class AdapterSums:
    def __init__(self, line, split, shared, adapters, slabs):
        full = shared[0][0].shape[-1]
        width = full // slabs
        self.line, self.split = line, split
        self.adapters, self.width = adapters, width
        self.n_shared = sum(x.size // full for x, _ in shared)
        n_split = sum(x.size // width for x, _ in split) + 16
        arrays = [x for pair in shared + split for x in pair]
        slab = (self.n_shared, width)
        far, beside, self.own, self.sent = line.call(
            functools.partial(wire_kernel, len(shared), len(shared) + len(split)),
            "wire",
            (1,),
            arrays,
            [whole(x) for x in arrays],
            tuple(
                jax.ShapeDtypeStruct(shape, BF16)
                for shape in ((2, *slab), slab, slab, (n_split, width))
            ),
            tuple(out_whole(shape) for shape in ((2, *slab), slab, slab, (n_split, width))),
            [pltpu.VMEM((self.n_shared, full), BF16)],
        )
        self.slab_sum = SlabSum(line, (far, beside, self.own))

    def cross(self):
        self.slab_sum.cross()

    def join(self):
        rows = self.own.shape[0] + self.sent.shape[0]
        ins = (*self.slab_sum.terms, self.sent)
        sent = self.line.call(
            join_kernel,
            "join",
            (1,),
            ins,
            [whole(x) for x in ins],
            jax.ShapeDtypeStruct((rows, self.width), BF16),
            out_whole((rows, self.width)),
        )
        self.everyone = lax.all_gather(sent, "dp", axis=0, tiled=False)

    def combine(self):
        shapes = [(self.adapters, x.size // x.shape[-1], x.shape[-1]) for x, _ in self.split]
        shared = (self.adapters, self.n_shared, self.width)
        shared, *split = self.line.call(
            functools.partial(combine_kernel, self.n_shared, self.adapters),
            "combine",
            (1,),
            (self.everyone,),
            [whole(self.everyone)],
            (
                jax.ShapeDtypeStruct(shared, BF16),
                *(jax.ShapeDtypeStruct(shape, F32) for shape in shapes),
            ),
            (out_whole(shared), *(out_whole(shape) for shape in shapes)),
        )
        self.parts = spread(shared.reshape(-1, self.width), "pair")
        return split


def on_device(
    slabs,
    tokens,
    cotangent,
    norm_gains,
    query_key_value_matrix,
    output_matrix,
    gate_up_matrix,
    down_matrix,
    lead_factors,
    head_factors,
    unit_factors,
    merge_factors,
    down_factors,
    tail_factors,
    doc_ids,
    keep_mask,
    adapter_pick,
):
    length = tokens.shape[1]
    rows = length // CHUNKS
    chosen = adapter_pick[0, 0]
    state = jnp.stack([lax.axis_index("tensor").astype(jnp.int32), chosen])
    line = Line(state)
    gains = norm_gains.astype(F32)
    lead = jnp.swapaxes(lead_factors, 2, 3)
    merge = jnp.swapaxes(merge_factors, 1, 2)
    down = jnp.swapaxes(down_factors, 1, 2)
    cosine, sine = rope_tables(length)
    doc_column = doc_ids.reshape(length, 1)

    def cut(array, c):
        return array[c * rows : (c + 1) * rows]

    own_tokens = [cut(tokens[0], c) for c in range(CHUNKS)]
    token_parts = [spread(own, MODES["tok"][c]) for c, own in enumerate(own_tokens)]
    own_cots = [cut(cotangent[0], c) for c in range(CHUNKS)]
    cot_parts = [spread(own, MODES["cot"][c]) for c, own in enumerate(own_cots)]

    def project_chunk(c, after=()):
        return project(
            line,
            token_parts[c],
            gains,
            lead,
            query_key_value_matrix,
            head_factors,
            cut(cosine, c),
            cut(sine, c),
            after,
        )

    def attend_chunk(c, qkvs, after=()):
        return attend(
            line,
            qkvs,
            c,
            doc_column,
            doc_ids,
            keep_mask,
            output_matrix,
            merge,
            tail_factors,
            slabs,
            MODES["branch"][c],
            after,
        )

    def feed_chunk(c, parts, after=()):
        return feed_forward(
            line,
            parts,
            cot_parts[c],
            gains,
            lead,
            gate_up_matrix,
            down_matrix,
            unit_factors,
            down,
            tail_factors,
            (MODES["feed"][c], MODES["back"][c]),
            after,
        )

    def attend_back_chunk(c, parts, after=()):
        return attend_back(
            line,
            parts,
            qkvs[: c + 1],
            c,
            doc_column,
            doc_ids,
            keep_mask,
            attended[c],
            output_matrix,
            merge,
            tail_factors,
            after,
        )

    def project_back_chunk(c, query_grad, later, after=()):
        normed, mid, scale = saved[c]
        return project_back(
            line,
            query_grad,
            later,
            c,
            query_key_value_matrix,
            head_factors,
            lead,
            gains,
            normed,
            mid,
            scale,
            cut(cosine, c),
            cut(sine, c),
            slabs,
            MODES["last"][c],
            after,
        )

    adapters = lead_factors.shape[1]
    qkv0, *saved0 = project_chunk(0)
    attended0, *branch0 = attend_chunk(0, [qkv0])
    branch0 = SlabSum(line, branch0)
    qkv1, *saved1 = project_chunk(1)
    qkvs, saved = [qkv0, qkv1], [saved0, saved1]
    attended1, *branch1 = attend_chunk(1, qkvs, tuple(cot_parts[0][1:4]))
    attended = [attended0, attended1]
    branch1 = SlabSum(line, branch1)
    hidden0, rounded0 = branch0.finish(own_tokens[0], tuple(cot_parts[0][4:]))
    hidden_parts0 = spread(rounded0, MODES["hidden"][0])
    branch1.cross(tuple(cot_parts[1][1:4]))
    hidden1, rounded1 = branch1.finish(own_tokens[1], tuple(cot_parts[1][4:]))
    hidden_parts1 = spread(rounded1, MODES["hidden"][1])
    feed0, back0, unit_grads0 = feed_chunk(0, hidden_parts0)
    back0 = SlabSum(line, back0)
    feed1, back1, unit_grads1 = feed_chunk(1, hidden_parts1)
    back1 = SlabSum(line, back1)
    grad0, rounded0 = back0.finish(own_cots[0])
    grad_parts0 = spread(rounded0, MODES["grad"][0])
    back1.cross()
    grad1, rounded1 = back1.finish(own_cots[1])
    grad_parts1 = spread(rounded1, MODES["grad"][1])
    feed0_far, feed0_beside, feed1_far, feed1_beside = relay(line, (*feed0[:2], *feed1[:2]))
    feed0 = SlabSum(line, [feed0_far, feed0_beside, feed0[2]])
    query_grad0, key_grad0, value_grad0, *merge_grads0 = attend_back_chunk(0, grad_parts0)
    early = AdapterSums(
        line,
        list(zip(unit_grads0, unit_grads1))[:2],
        list(zip(unit_grads0, unit_grads1))[2:],
        adapters,
        slabs,
    )
    feed0.cross()
    feed1 = SlabSum(line, [feed1_far, feed1_beside, feed1[2]])
    query_grad1, key_grad1, value_grad1, *merge_grads1 = attend_back_chunk(1, grad_parts1)
    early.cross()
    feed1.cross()
    last1, *head_grads1 = project_back_chunk(1, query_grad1, [key_grad1, value_grad1])
    last1 = SlabSum(line, last1)
    early.join()
    _, out0 = feed0.finish(hidden0)
    last0, *head_grads0 = project_back_chunk(
        0, query_grad0, [key_grad0, value_grad0, key_grad1, value_grad1]
    )
    last0 = SlabSum(line, last0)
    (head0, lead0), (head1, lead1) = head_grads0, head_grads1
    (merge0, tail0), (merge1, tail1) = merge_grads0, merge_grads1
    late = AdapterSums(
        line,
        [(head0, head1), (merge0, merge1)],
        [(lead0, lead1), (tail0, tail1)],
        adapters,
        slabs,
    )
    layer_out = feed1.finish_after(hidden1, out0)
    late.cross()
    late.join()
    last0.cross()
    unit_all, down_all = early.combine()
    _, tokens_grad1 = last1.finish(grad1)
    head_all, merge_all = late.combine()
    _, tokens_grad0 = last0.finish(grad0)
    rank = lead_factors.shape[3]
    lead_all, tail_all = whole_width(line, early.parts, late.parts, adapters, rank)

    def ranked(array):
        return jnp.swapaxes(array.reshape(adapters, -1, rank, array.shape[-1]), 0, 1)

    return (
        layer_out[None],
        jnp.concatenate([tokens_grad0, tokens_grad1])[None],
        jnp.swapaxes(lead_all, 2, 3),
        ranked(head_all),
        ranked(unit_all),
        jnp.swapaxes(merge_all, 1, 2),
        jnp.swapaxes(down_all, 1, 2),
        tail_all,
    )


def solution(mesh):
    return jax.shard_map(
        functools.partial(on_device, mesh.shape["tensor"]),
        mesh=mesh,
        in_specs=(
            P("dp", None, "tensor"),
            P("dp", None, "tensor"),
            P(),
            P(None, None, "tensor"),
            P("tensor", None),
            P(None, None, "tensor"),
            P("tensor", None),
            P(),
            P(None, None, None, "tensor"),
            P(None, None, None, "tensor"),
            P(None, "tensor", None),
            P(None, "tensor", None),
            P(),
            P("dp", None),
            P("dp", None),
            P("dp", None),
        ),
        out_specs=(
            P("dp", None, "tensor"),
            P("dp", None, "tensor"),
            P(),
            P(None, None, None, "tensor"),
            P(None, None, None, "tensor"),
            P(None, "tensor", None),
            P(None, "tensor", None),
            P(),
        ),
        check_vma=False,
    )
```

```python
import functools
import math

import jax
import jax.numpy as jnp
from jax import lax
from jax.experimental import pallas as pl
from jax.experimental.pallas import tpu as pltpu
from jax.sharding import PartitionSpec as P

HEAD_DIM = 64
EPSILON = 1e-05
ROPE_BASE = 130000.0
SCALING = 2.0
MASKED = -1000000000.0
LONGEST_DOC = 512
CHUNKS = 2
MODES = {
    "tok": "stack",
    "cot": "stack",
    "branch": ("pair", "pair"),
    "hidden": ("stack", "stack"),
    "feed": ("pair", "stack"),
    "back": ("stack", "pair"),
    "grad": ("stack", "stack"),
    "last": ("pair", "pair"),
}
SUB_ROWS = 256
LARGE_VMEM = 60 * 1024 * 1024
SMALL_VMEM = 30 * 1024 * 1024

BESIDE = [(0, 1), (1, 0), (2, 3), (3, 2)]
MIDDLE = [(1, 2), (2, 1)]
OVER = [(0, 2), (3, 1)]
ACROSS = [(1, 3), (2, 0)]
OUTWARD = [(1, 0), (2, 3)]
INWARD = [(0, 1), (3, 2)]

F32 = jnp.float32
BF16 = jnp.bfloat16


def dot(a, b):
    return jnp.dot(a, b, preferred_element_type=F32)


def dot_nt(a, b):
    return lax.dot_general(a, b, (((1,), (1,)), ((), ())), preferred_element_type=F32)


def dot_tn(a, b):
    return lax.dot_general(a, b, (((0,), (0,)), ((), ())), preferred_element_type=F32)


def whole(array):
    rank = len(array.shape)
    return pl.BlockSpec(array.shape, lambda *_: (0,) * rank, pipeline_mode=pl.Buffered(1))


ANY = pl.BlockSpec(memory_space=pl.ANY)


def out_whole(shape):
    rank = len(shape)
    return pl.BlockSpec(shape, lambda *_: (0,) * rank)


def spread(own, mode):
    if mode == "stack":
        return [lax.all_gather(own, "tensor", axis=0, tiled=False)]
    beside = lax.ppermute(own, "tensor", BESIDE)
    near = lax.ppermute(own, "tensor", MIDDLE)
    far = lax.ppermute(own, "tensor", OVER)
    return [
        own,
        beside,
        near,
        far,
        lax.ppermute(near, "tensor", OUTWARD),
        lax.ppermute(far, "tensor", OUTWARD),
    ]


def slab_columns(slab, width):
    return pl.ds(pl.multiple_of(slab * width, width), width)


def slab_copies(state, parts, target, sems, first=0):
    here = pl.ds(first, target.shape[0])
    width = parts[0].shape[-1]
    if len(parts) == 1:
        return [
            (None, pltpu.make_async_copy(
                parts[0].at[j, here], target.at[:, j * width : (j + 1) * width], sems.at[j]
            ))
            for j in range(parts[0].shape[0])
        ]
    me, inner, near, far = places(state)
    copies = []
    for sem, (condition, part, slab) in enumerate((
        (None, parts[0], me),
        (None, parts[1], beside_of(me)),
        (inner, parts[2], near),
        (inner, parts[3], far),
        (jnp.logical_not(inner), parts[4], near),
        (jnp.logical_not(inner), parts[5], far),
    )):
        copies.append((condition, pltpu.make_async_copy(
            part.at[here], target.at[:, slab_columns(slab, width)], sems.at[sem % 4 + 2 * (sem // 4)]
        )))
    return copies


def beside_of(me):
    return me + 1 - 2 * lax.rem(me, 2)


def places(state):
    me = state[0]
    upper = me >= 2
    return me, (me == 1) | (me == 2), jnp.where(upper, 1, 2), jnp.where(upper, 0, 3)


def each_copy(copies, act):
    for condition, copy in copies:
        if condition is None:
            act(copy)
        else:
            pl.when(condition)(functools.partial(act, copy))


def start_copies(copies):
    each_copy(copies, lambda copy: copy.start())


def wait_copies(copies):
    each_copy(copies, lambda copy: copy.wait())


def write_slabs(state, outs, term):
    width = outs[0].shape[-1]
    if len(outs) == 1:
        for slab in range(outs[0].shape[0]):
            outs[0][slab] = term(slab_columns(slab, width)).astype(BF16)
        return
    me, _, near, far = places(state)
    for target, slab in (
        (outs[0].at[0], near),
        (outs[0].at[1], far),
        (outs[1], beside_of(me)),
        (outs[2], me),
    ):
        target[...] = term(slab_columns(slab, width)).astype(BF16)


def slab_outs(mode, count, rows, width):
    if mode == "stack":
        shapes = ((count, rows, width),)
    else:
        shapes = ((2, rows, width), (rows, width), (rows, width))
    return (
        tuple(jax.ShapeDtypeStruct(shape, BF16) for shape in shapes),
        tuple(out_whole(shape) for shape in shapes),
    )


def add_kernel(state, far, received, beside, near_out, far_out, beside_out):
    near_out[...] = (far[0].astype(F32) + received[0].astype(F32)).astype(BF16)
    far_out[...] = (far[1].astype(F32) + received[1].astype(F32)).astype(BF16)
    beside_out[...] = beside[...]


def sum_kernel(state, *refs):
    terms, (exact, rounded) = refs[:-2], refs[-2:]
    total = terms[0][...].astype(F32)
    for term in terms[1:]:
        total += term[...].astype(F32)
    exact[...] = total
    rounded[...] = total.astype(BF16)


def sum_beside_kernel(chunk, count, state, other, *refs):
    terms, joined = refs[:-1], refs[-1]
    here = pl.program_id(0) // count == chunk

    @pl.when(jnp.logical_not(here))
    def _():
        joined[...] = other[...]

    @pl.when(here)
    def _():
        total = terms[0][...].astype(F32)
        for term in terms[1:]:
            total += term[...].astype(F32)
        joined[...] = total.astype(BF16)


def relay_kernel(state, *refs):
    count = len(refs) // 2
    for source, target in zip(refs[:count], refs[count:]):
        target[...] = source[...]


def relay(line, parts, after=()):
    return line.call(
        relay_kernel,
        "relay",
        (1,),
        parts,
        [whole(x) for x in parts],
        tuple(jax.ShapeDtypeStruct(x.shape, x.dtype) for x in parts),
        tuple(out_whole(x.shape) for x in parts),
        after=after,
    )


class SlabSum:
    def __init__(self, line, parts):
        self.line, self.parts = line, parts
        if len(parts) == 1:
            self.terms = [
                lax.psum_scatter(parts[0], "tensor", scatter_dimension=0, tiled=False)
            ]
        else:
            self.received = lax.ppermute(parts[0], "tensor", INWARD)

    def cross(self, after=()):
        far, beside, own = self.parts
        rows, width = own.shape
        step = min(256, rows)
        flat = pl.BlockSpec((step, width), lambda i, s: (i, 0))
        both = pl.BlockSpec((2, step, width), lambda i, s: (0, i, 0))
        near, far, beside = self.line.call(
            add_kernel,
            "add",
            (rows // step,),
            (far, self.received, beside),
            [both, both, flat],
            (jax.ShapeDtypeStruct((rows, width), BF16),) * 3,
            (flat,) * 3,
            after=after,
        )
        near = lax.ppermute(near, "tensor", MIDDLE)
        far = lax.ppermute(far, "tensor", ACROSS)
        beside = lax.ppermute(beside, "tensor", BESIDE)
        self.terms = [own, beside, near, far]

    def finish(self, base, after=()):
        rows, width = base.shape
        step = min(256, rows)
        flat = pl.BlockSpec((step, width), lambda i, s: (i, 0))
        return self.line.call(
            sum_kernel,
            "sum",
            (rows // step,),
            (base, *self.terms),
            [flat] * (1 + len(self.terms)),
            (jax.ShapeDtypeStruct((rows, width), F32), jax.ShapeDtypeStruct((rows, width), BF16)),
            (flat, flat),
            after=after,
        )


    def finish_beside(self, base, other, chunk):
        rows, width = base.shape
        step = min(256, rows)
        count = rows // step

        def rows_of(c):
            return pl.BlockSpec(
                (step, width), lambda i, s: (jnp.clip(i - c * count, 0, count - 1), 0)
            )

        return self.line.call(
            functools.partial(sum_beside_kernel, chunk, count),
            "sum_beside",
            (2 * count,),
            (other, base, *self.terms),
            [rows_of(1 - chunk)] + [rows_of(chunk)] * (1 + len(self.terms)),
            jax.ShapeDtypeStruct((2 * rows, width), BF16),
            pl.BlockSpec((step, width), lambda i, s: (i, 0)),
        )


def params(name):
    return pltpu.CompilerParams(
        dimension_semantics=("arbitrary",),
        vmem_limit_bytes=LARGE_VMEM if name == "feed_forward" else SMALL_VMEM,
    )


class Line:
    def __init__(self, state):
        self.state, self.last = state, ()

    def call(self, kernel, name, grid, ins, in_specs, outs, out_specs, scratch=(), after=()):
        after = (*self.last, *after)
        n_used = 1 + len(ins)

        def body(*refs):
            kernel(*refs[:n_used], *refs[n_used + len(after) :])

        results = pl.pallas_call(
            body,
            name=name,
            grid_spec=pltpu.PrefetchScalarGridSpec(
                num_scalar_prefetch=1,
                grid=grid,
                in_specs=list(in_specs) + [ANY] * len(after),
                out_specs=out_specs,
                scratch_shapes=list(scratch),
            ),
            out_shape=outs,
            compiler_params=params(name),
            cost_estimate=pl.CostEstimate(flops=1, bytes_accessed=1, transcendentals=0),
        )(self.state, *ins, *after)
        self.last = (jax.tree.leaves(results)[-1],)
        return results


def swap_halves(values):
    width = values.shape[-1]
    half = HEAD_DIM // 2
    lane = lax.broadcasted_iota(jnp.int32, values.shape, values.ndim - 1) % HEAD_DIM
    return jnp.where(
        lane < half,
        pltpu.roll(values, width - half, values.ndim - 1),
        pltpu.roll(values, half, values.ndim - 1),
    )


def rope_groups(values, cosine, sine, sign):
    groups = []
    for first in range(0, values.shape[-1], 128):
        group = values[:, first : first + 128]
        groups.append(group * cosine + (sign * swap_halves(group)) * sine)
    return jnp.concatenate(groups, axis=-1)


def project_kernel(first_row, n_parts, state, *refs):
    parts, refs = refs[:n_parts], refs[n_parts:]
    gain, lead, weight, head, cosine, sine, qkv, normed, mid, scale, stream, sems = refs
    step = pl.program_id(0)
    rank = lead.shape[2]

    @pl.when(step == 0)
    def _():
        copies = slab_copies(state, parts, stream, sems, first_row)
        start_copies(copies)
        wait_copies(copies)
        for first in range(0, stream.shape[0], SUB_ROWS):
            here = pl.ds(first, SUB_ROWS)
            rows = stream[here, :].astype(F32)
            r1 = lax.rsqrt(jnp.mean(rows * rows, axis=1, keepdims=True) + EPSILON)
            scale[here, :] = r1
            values = (rows * r1 * gain[0:1, :]).astype(BF16)
            normed[here, :] = values
            mids = dot_nt(values, lead[:3, 0].reshape(3 * rank, -1))
            for j in range(3):
                mid[j, here, :] = mids[:, j * rank : (j + 1) * rank].astype(BF16)

    for first in range(0, stream.shape[0], SUB_ROWS):
        here = pl.ds(first, SUB_ROWS)
        projected = dot(normed[here, :], weight[0]) + SCALING * dot(mid[step, here, :], head[0, 0])

        @pl.when(step < 2)
        def _():
            qkv[0, here, :] = rope_groups(projected, cosine[here, :], sine[here, :], 1.0).astype(BF16)

        @pl.when(step == 2)
        def _():
            qkv[0, here, :] = projected.astype(BF16)


def project(line, parts, chunk, gains, lead, weight, head, cosine, sine, after=()):
    rows = cosine.shape[0]
    full, width = weight.shape[1:]
    rank = lead.shape[2]
    slabs = full // parts[0].shape[-1]
    return line.call(
        functools.partial(project_kernel, chunk * rows, len(parts)),
        "project",
        (3,),
        (*parts, gains, lead, weight, head, cosine, sine),
        [ANY] * len(parts)
        + [
            whole(gains),
            pl.BlockSpec(
                (lead.shape[0], 1, rank, full),
                lambda j, s: (0, s[1], 0, 0),
                pipeline_mode=pl.Buffered(1),
            ),
            pl.BlockSpec((1, full, width), lambda j, s: (j, 0, 0)),
            pl.BlockSpec((1, 1, rank, width), lambda j, s: (j, s[1], 0, 0)),
            whole(cosine),
            whole(sine),
        ],
        (
            jax.ShapeDtypeStruct((3, rows, width), BF16),
            jax.ShapeDtypeStruct((rows, full), BF16),
            jax.ShapeDtypeStruct((3, rows, rank), BF16),
            jax.ShapeDtypeStruct((rows, 1), F32),
        ),
        (
            pl.BlockSpec((1, rows, width), lambda j, s: (j, 0, 0)),
            out_whole((rows, full)),
            out_whole((3, rows, rank)),
            out_whole((rows, 1)),
        ),
        [pltpu.VMEM((rows, full), BF16), pltpu.SemaphoreType.DMA((slabs,))],
        after,
    )


def head_mask(shape, half):
    lane = lax.broadcasted_iota(jnp.int32, shape, len(shape) - 1)
    return (lane >= HEAD_DIM) if half else (lane < HEAD_DIM)


def key_span(first_row, block):
    low = max(0, first_row - LONGEST_DOC + 1)
    return (low // 128) * 128, first_row + block


def key_bias(doc_rows, doc_keys, keep_keys, first_row, low, high, block):
    rows_at = first_row + lax.broadcasted_iota(jnp.int32, (block, high - low), 0)
    keys_at = low + lax.broadcasted_iota(jnp.int32, (block, high - low), 1)
    same = doc_rows == doc_keys[:, low:high]
    live = (keep_keys[:, low:high] == 1) | (rows_at == keys_at)
    return jnp.where((keys_at <= rows_at) & same & live, 0.0, MASKED)


def attend_kernel(first_row, block, n_chunks, n_outs, state, *refs):
    chunks, refs = refs[: 2 * n_chunks], refs[2 * n_chunks :]
    query, doc_rows, doc_keys, keep, weight, merge, tail = refs[:7]
    attended, refs = refs[7], refs[8:]
    branch, (keys, values, bias, held) = refs[:n_outs], refs[n_outs:]
    step = pl.program_id(0)
    rows = query.shape[1]
    for c in range(n_chunks):
        keys[c * rows : (c + 1) * rows, :] = chunks[2 * c][0]
        values[c * rows : (c + 1) * rows, :] = chunks[2 * c + 1][0]
    for sub in range(rows // block):
        start = first_row + sub * block
        low, high = key_span(start, block)
        here = pl.ds(sub * block, block)

        @pl.when(step == 0)
        def _():
            bias[sub, :, : high - low] = key_bias(
                doc_rows[here, :], doc_keys[...], keep[...], start, low, high, block
            )

        outs = []
        for half in range(2):
            mask = head_mask((block, 128), half)
            q = jnp.where(mask, query[0, here, :] * (HEAD_DIM**-0.5), 0.0).astype(BF16)
            scores = dot_nt(q, keys[low:high, :]) + bias[sub, :, : high - low]
            raised = jnp.exp(scores - jnp.max(scores, axis=1, keepdims=True))
            total = jnp.sum(raised, axis=1, keepdims=True)
            weights = (raised * (1.0 / total)).astype(BF16)
            outs.append(dot(weights, values[low:high, :]))
        columns = pl.ds(pl.multiple_of(step * 128, 128), 128)
        held[here, columns] = jnp.where(head_mask((block, 128), 0), outs[0], outs[1]).astype(BF16)

    @pl.when(step == pl.num_programs(0) - 1)
    def _():
        result = held[...]
        attended[...] = result
        mid = dot_nt(result, merge[0]).astype(BF16)
        write_slabs(
            state,
            branch,
            lambda columns: dot(result, weight[:, columns])
            + SCALING * dot(mid, tail[0, 0, :, columns]),
        )


def attend(line, qkvs, chunk, doc_column, doc_row, keep_row, weight, merge, tail, slabs, mode, after=()):
    rows, width = qkvs[0].shape[1:]
    first_row = chunk * rows
    block = min(256, rows)
    n_chunks = chunk + 1
    rank, full = merge.shape[1], weight.shape[1]
    ins, specs = [], []
    for c in range(n_chunks):
        for j in (1, 2):
            ins.append(qkvs[c])
            specs.append(pl.BlockSpec((1, rows, 128), lambda i, s, j=j: (j, 0, i)))
    ins += [qkvs[chunk], doc_column, doc_row, keep_row, weight, merge, tail]
    specs += [
        pl.BlockSpec((1, rows, 128), lambda i, s: (0, 0, i)),
        pl.BlockSpec((rows, 1), lambda i, s: (chunk, 0), pipeline_mode=pl.Buffered(1)),
        whole(doc_row),
        whole(keep_row),
        whole(weight),
        pl.BlockSpec((1, rank, width), lambda i, s: (s[1], 0, 0), pipeline_mode=pl.Buffered(1)),
        pl.BlockSpec(
            (1, 1, rank, full), lambda i, s: (0, s[1], 0, 0), pipeline_mode=pl.Buffered(1)
        ),
    ]
    n_keys = first_row + rows
    shapes, out_specs = slab_outs(mode, slabs, rows, full // slabs)
    outs = line.call(
        functools.partial(attend_kernel, first_row, block, n_chunks, len(shapes)),
        "attend",
        (width // 128,),
        ins,
        specs,
        (jax.ShapeDtypeStruct((rows, width), BF16),) + shapes,
        (out_whole((rows, width)),) + out_specs,
        [
            pltpu.VMEM((n_keys, 128), BF16),
            pltpu.VMEM((n_keys, 128), BF16),
            pltpu.VMEM((rows // block, block, min(n_keys, LONGEST_DOC + block)), F32),
            pltpu.VMEM((rows, width), BF16),
        ],
        after,
    )
    return outs


def feed_kernel(first_row, n_parts, n_cots, n_feed, n_back, state, *refs):
    parts, refs = refs[:n_parts], refs[n_parts:]
    cot_parts, refs = refs[:n_cots], refs[n_cots:]
    gain, lead, gate_w, up_w, down_w, unit, down, tail = refs[:8]
    refs = refs[8:]
    feed, refs = refs[:n_feed], refs[n_feed:]
    back, refs = refs[:n_back], refs[n_back:]
    unit_grad, down_grad, lead_grad, tail_grad = refs[:4]
    stream, upstream, normed, mid, down_back, scale = refs[4:10]
    feed_sum, back_sum, down_mid, unit_back, sems, cot_sems = refs[10:]
    step = pl.program_id(0)
    rank = lead.shape[2]
    firsts = range(0, stream.shape[0], SUB_ROWS)

    @pl.when(step == 0)
    def _():
        copies = slab_copies(state, parts, stream, sems)
        cot_copies = slab_copies(state, cot_parts, upstream, cot_sems, first_row)
        start_copies(copies)
        start_copies(cot_copies)
        wait_copies(copies)
        for first in firsts:
            here = pl.ds(first, SUB_ROWS)
            rows = stream[here, :].astype(F32)
            r2 = lax.rsqrt(jnp.mean(rows * rows, axis=1, keepdims=True) + EPSILON)
            scale[here, :] = r2
            values = (rows * r2 * gain[1:2, :]).astype(BF16)
            normed[here, :] = values
            mids = dot_nt(values, lead[3:5, 0].reshape(2 * rank, -1))
            for j in range(2):
                mid[j, here, :] = mids[:, j * rank : (j + 1) * rank].astype(BF16)
        wait_copies(cot_copies)
        down_back[...] = (SCALING * dot_nt(upstream[...], tail[0, 0])).astype(BF16)
        feed_sum[...] = jnp.zeros_like(feed_sum)
        back_sum[...] = jnp.zeros_like(back_sum)
        down_mid[...] = jnp.zeros_like(down_mid)
        unit_back[...] = jnp.zeros_like(unit_back)

    unit_terms = [0.0, 0.0]
    down_term = 0.0
    for first in firsts:
        here = pl.ds(first, SUB_ROWS)
        gate = dot(normed[here, :], gate_w[0]) + SCALING * dot(mid[0, here, :], unit[0, 0])
        up = dot(normed[here, :], up_w[0]) + SCALING * dot(mid[1, here, :], unit[1, 0])
        hidden_grad = dot_nt(upstream[here, :], down_w[...]) + dot(down_back[here, :], down[0])
        sigma = 1.0 / (1.0 + jnp.exp(-gate))
        active = gate * sigma
        hidden = (active * up).astype(BF16)
        up_grad = (hidden_grad * active).astype(BF16)
        gate_grad = (hidden_grad * up * (sigma + active * (1.0 - sigma))).astype(BF16)
        feed_sum[here, :] += dot(hidden, down_w[...])
        back_sum[here, :] += dot_nt(gate_grad, gate_w[0]) + dot_nt(up_grad, up_w[0])
        down_mid[here, :] += dot_nt(hidden, down[0])
        unit_back[0, here, :] += dot_nt(gate_grad, unit[0, 0])
        unit_back[1, here, :] += dot_nt(up_grad, unit[1, 0])
        unit_terms[0] += dot_tn(mid[0, here, :], gate_grad)
        unit_terms[1] += dot_tn(mid[1, here, :], up_grad)
        down_term += dot_tn(down_back[here, :], hidden)
    unit_grad[0] = SCALING * unit_terms[0]
    unit_grad[1] = SCALING * unit_terms[1]
    down_grad[...] = down_term

    @pl.when(step == pl.num_programs(0) - 1)
    def _():
        values = normed[...]
        mid_down = down_mid[...].astype(BF16)
        tail_grad[...] = SCALING * dot_tn(mid_down, upstream[...])
        unit_backs = [(SCALING * unit_back[j]).astype(BF16) for j in range(2)]
        for j in range(2):
            lead_grad[j] = dot_tn(unit_backs[j], values)
        write_slabs(
            state,
            feed,
            lambda columns: feed_sum[:, columns] + SCALING * dot(mid_down, tail[0, 0, :, columns]),
        )
        for first in firsts:
            here = pl.ds(first, SUB_ROWS)
            there = slice(first, first + SUB_ROWS)
            r2 = scale[here, :]
            total = back_sum[here, :]
            for j in range(2):
                total += dot(unit_backs[j][there], lead[3 + j, 0])
            inner = jnp.mean(total * normed[here, :].astype(F32), axis=1, keepdims=True)
            back_sum[here, :] = r2 * (
                gain[1:2, :] * total - stream[here, :].astype(F32) * (r2 * inner)
            )
        write_slabs(state, back, lambda columns: back_sum[:, columns])


def feed_forward(
    line, parts, cot_parts, chunk, gains, lead, gate_up, down_w, unit, down, tail, modes, after=()
):
    feed_mode, back_mode = modes
    rows, slab_width = parts[0].shape[-2:]
    full, units = gate_up.shape[1:]
    rank = lead.shape[2]
    slabs = full // slab_width
    block = min(512, units)
    feed_shapes, feed_specs = slab_outs(feed_mode, slabs, rows, slab_width)
    back_shapes, back_specs = slab_outs(back_mode, slabs, rows, slab_width)
    outs = line.call(
        functools.partial(
            feed_kernel, chunk * rows, len(parts), len(cot_parts), len(feed_shapes), len(back_shapes)
        ),
        "feed_forward",
        (units // block,),
        (*parts, *cot_parts, gains, lead, gate_up, gate_up, down_w, unit, down, tail),
        [ANY] * (len(parts) + len(cot_parts))
        + [
            whole(gains),
            pl.BlockSpec(
                (lead.shape[0], 1, rank, full),
                lambda i, s: (0, s[1], 0, 0),
                pipeline_mode=pl.Buffered(1),
            ),
            pl.BlockSpec((1, full, block), lambda i, s: (0, 0, i)),
            pl.BlockSpec((1, full, block), lambda i, s: (1, 0, i)),
            pl.BlockSpec((block, full), lambda i, s: (i, 0)),
            pl.BlockSpec((2, 1, rank, block), lambda i, s: (0, s[1], 0, i)),
            pl.BlockSpec((1, rank, block), lambda i, s: (s[1], 0, i)),
            pl.BlockSpec(
                (1, 1, rank, full), lambda i, s: (1, s[1], 0, 0), pipeline_mode=pl.Buffered(1)
            ),
        ],
        feed_shapes
        + back_shapes
        + (
            jax.ShapeDtypeStruct((2, rank, units), F32),
            jax.ShapeDtypeStruct((rank, units), F32),
            jax.ShapeDtypeStruct((2, rank, full), F32),
            jax.ShapeDtypeStruct((rank, full), F32),
        ),
        feed_specs
        + back_specs
        + (
            pl.BlockSpec((2, rank, block), lambda i, s: (0, 0, i)),
            pl.BlockSpec((rank, block), lambda i, s: (0, i)),
            out_whole((2, rank, full)),
            out_whole((rank, full)),
        ),
        [
            pltpu.VMEM((rows, full), BF16),
            pltpu.VMEM((rows, full), BF16),
            pltpu.VMEM((rows, full), BF16),
            pltpu.VMEM((2, rows, rank), BF16),
            pltpu.VMEM((rows, rank), BF16),
            pltpu.VMEM((rows, 1), F32),
            pltpu.VMEM((rows, full), F32),
            pltpu.VMEM((rows, full), F32),
            pltpu.VMEM((rows, rank), F32),
            pltpu.VMEM((2, rows, rank), F32),
            pltpu.SemaphoreType.DMA((slabs,)),
            pltpu.SemaphoreType.DMA((slabs,)),
        ],
        after,
    )
    n_feed, n_both = len(feed_shapes), len(feed_shapes) + len(back_shapes)
    return list(outs[:n_feed]), list(outs[n_feed:n_both]), outs[n_both:]


def attend_back_kernel(first_row, block, n_chunks, n_parts, state, *refs):
    parts, refs = refs[:n_parts], refs[n_parts:]
    chunks, refs = refs[: 2 * n_chunks], refs[2 * n_chunks :]
    query, doc_rows, doc_keys, keep, attended, weight, merge, tail = refs[:8]
    query_grad, key_grad, value_grad, merge_grad, tail_grad = refs[8:13]
    keys, values, bias, branch, out_grad, sems = refs[13:]
    step = pl.program_id(0)
    rows = query.shape[1]
    inverse_root = HEAD_DIM**-0.5

    @pl.when(step == 0)
    def _():
        copies = slab_copies(state, parts, branch, sems)
        start_copies(copies)
        wait_copies(copies)
        gradient = branch[...]
        result = attended[...]
        merge_back = (SCALING * dot_nt(gradient, tail[0, 0])).astype(BF16)
        merge_mid = dot_nt(result, merge[0]).astype(BF16)
        merge_grad[...] = dot_tn(merge_back, result)
        tail_grad[...] = SCALING * dot_tn(merge_mid, gradient)
        whole_grad = (dot_nt(gradient, weight[...]) + dot(merge_back, merge[0])).astype(BF16)
        for pair in range(out_grad.shape[0]):
            out_grad[pair] = whole_grad[:, pair * 128 : (pair + 1) * 128]

    for c in range(n_chunks):
        keys[c * rows : (c + 1) * rows, :] = chunks[2 * c][0]
        values[c * rows : (c + 1) * rows, :] = chunks[2 * c + 1][0]
    key_grad[...] = jnp.zeros_like(key_grad)
    value_grad[...] = jnp.zeros_like(value_grad)
    for sub in range(rows // block):
        start = first_row + sub * block
        low, high = key_span(start, block)
        here = pl.ds(sub * block, block)

        @pl.when(step == 0)
        def _():
            bias[sub, :, : high - low] = key_bias(
                doc_rows[here, :], doc_keys[...], keep[...], start, low, high, block
            )

        outs = []
        key_term = value_term = 0.0
        for half in range(2):
            mask = head_mask((block, 128), half)
            q = jnp.where(mask, query[0, here, :] * inverse_root, 0.0).astype(BF16)
            grad = jnp.where(mask, out_grad[step, here, :], 0.0).astype(BF16)
            scores = dot_nt(q, keys[low:high, :]) + bias[sub, :, : high - low]
            raised = jnp.exp(scores - jnp.max(scores, axis=1, keepdims=True))
            probs = raised * (1.0 / jnp.sum(raised, axis=1, keepdims=True))
            prob_grad = dot_nt(grad, values[low:high, :])
            inner = jnp.sum(probs * prob_grad, axis=1, keepdims=True)
            score_grad = (probs * (prob_grad - inner)).astype(BF16)
            outs.append(dot(score_grad, keys[low:high, :]))
            key_term += dot_tn(score_grad, q)
            value_term += dot_tn(probs.astype(BF16), grad)
        mixed = jnp.where(head_mask((block, 128), 0), outs[0], outs[1])
        query_grad[here, :] = mixed * inverse_root
        key_grad[low:high, :] += key_term
        value_grad[low:high, :] += value_term


def attend_back(line, parts, qkvs, chunk, doc_column, doc_row, keep_row, attended, weight, merge, tail, after=()):
    rows, width = qkvs[0].shape[1:]
    first_row = chunk * rows
    block = min(256, rows)
    n_chunks = chunk + 1
    rank, full = merge.shape[1], weight.shape[1]
    slabs = full // parts[0].shape[-1]
    ins, specs = list(parts), [ANY] * len(parts)
    for c in range(n_chunks):
        for j in (1, 2):
            ins.append(qkvs[c])
            specs.append(pl.BlockSpec((1, rows, 128), lambda i, s, j=j: (j, 0, i)))
    ins += [qkvs[chunk], doc_column, doc_row, keep_row, attended, weight, merge, tail]
    specs += [
        pl.BlockSpec((1, rows, 128), lambda i, s: (0, 0, i)),
        pl.BlockSpec((rows, 1), lambda i, s: (chunk, 0), pipeline_mode=pl.Buffered(1)),
        whole(doc_row),
        whole(keep_row),
        whole(attended),
        whole(weight),
        pl.BlockSpec((1, rank, width), lambda i, s: (s[1], 0, 0), pipeline_mode=pl.Buffered(1)),
        pl.BlockSpec(
            (1, 1, rank, full), lambda i, s: (0, s[1], 0, 0), pipeline_mode=pl.Buffered(1)
        ),
    ]
    n_keys = first_row + rows
    return line.call(
        functools.partial(attend_back_kernel, first_row, block, n_chunks, len(parts)),
        "attend_back",
        (width // 128,),
        ins,
        specs,
        (
            jax.ShapeDtypeStruct((rows, width), F32),
            jax.ShapeDtypeStruct((n_keys, width), F32),
            jax.ShapeDtypeStruct((n_keys, width), F32),
            jax.ShapeDtypeStruct((rank, width), F32),
            jax.ShapeDtypeStruct((rank, full), F32),
        ),
        (
            pl.BlockSpec((rows, 128), lambda i, s: (0, i)),
            pl.BlockSpec((n_keys, 128), lambda i, s: (0, i)),
            pl.BlockSpec((n_keys, 128), lambda i, s: (0, i)),
            out_whole((rank, width)),
            out_whole((rank, full)),
        ),
        [
            pltpu.VMEM((n_keys, 128), BF16),
            pltpu.VMEM((n_keys, 128), BF16),
            pltpu.VMEM((rows // block, block, min(n_keys, LONGEST_DOC + block)), F32),
            pltpu.VMEM((rows, full), BF16),
            pltpu.VMEM((width // 128, rows, 128), BF16),
            pltpu.SemaphoreType.DMA((slabs,)),
        ],
        after,
    )


def head_back_kernel(state, *refs):
    query_grads, key_grads, value_grads = refs[0:2], refs[2:4], refs[4:6]
    normed, mids = refs[6:8], refs[8:10]
    head, cosine, sine = refs[10:13]
    gradients, backs, head_grad, lead_grad = refs[13:]
    rows = query_grads[0].shape[0]
    rank = head.shape[2]
    head_terms = [jnp.zeros(head_grad.shape[1:], F32) for _ in range(3)]
    lead_term = jnp.zeros((3 * rank, lead_grad.shape[2]), F32)
    for c in range(2):
        for first in range(0, rows, SUB_ROWS):
            here = pl.ds(first, SUB_ROWS)
            there = pl.ds(c * rows + first, SUB_ROWS)
            key, value = key_grads[1][there, :], value_grads[1][there, :]
            if c == 0:
                key, value = key + key_grads[0][here, :], value + value_grads[0][here, :]
            tables = cosine[there, :], sine[there, :], -1.0
            turned = (
                rope_groups(query_grads[c][here, :], *tables),
                rope_groups(key, *tables),
                value,
            )
            back = []
            for j in range(3):
                gradient = turned[j].astype(BF16)
                gradients[j, there, :] = gradient
                back.append((SCALING * dot_nt(gradient, head[j, 0])).astype(BF16))
                backs[j, there, :] = back[j]
                head_terms[j] += dot_tn(mids[c][j, here, :], gradient)
            lead_term += dot_tn(jnp.concatenate(back, axis=1), normed[c][here, :])
    for j in range(3):
        head_grad[j] = SCALING * head_terms[j]
        lead_grad[j] = lead_term[j * rank : (j + 1) * rank]


def head_back(line, query_grads, key_grads, value_grads, saved, head, cosine, sine):
    rows, width = query_grads[0].shape
    full = saved[0][0].shape[1]
    rank = head.shape[2]
    ins = (
        *query_grads,
        *key_grads,
        *value_grads,
        *(normed for normed, _, _ in saved),
        *(mid for _, mid, _ in saved),
    )
    shapes = (
        ((3, 2 * rows, width), BF16),
        ((3, 2 * rows, rank), BF16),
        ((3, rank, width), F32),
        ((3, rank, full), F32),
    )
    return line.call(
        head_back_kernel,
        "head_back",
        (1,),
        (*ins, head, cosine, sine),
        [whole(x) for x in ins]
        + [
            pl.BlockSpec(
                (3, 1, rank, width), lambda i, s: (0, s[1], 0, 0), pipeline_mode=pl.Buffered(1)
            ),
            whole(cosine),
            whole(sine),
        ],
        tuple(jax.ShapeDtypeStruct(*shape) for shape in shapes),
        tuple(out_whole(shape) for shape, _ in shapes),
    )


def project_back_kernel(state, gradient, back, weight, lead, gain, normed, scale, *refs):
    outs, total = refs[:-1], refs[-1]
    step = pl.program_id(0)
    for first in range(0, total.shape[0], SUB_ROWS):
        here = pl.ds(first, SUB_ROWS)
        term = dot_nt(gradient[0, here, :], weight[0]) + dot(back[0, here, :], lead[0, 0])

        @pl.when(step == 0)
        def _():
            total[here, :] = term

        @pl.when(step > 0)
        def _():
            total[here, :] += term

    @pl.when(step == pl.num_programs(0) - 1)
    def _():
        for first in range(0, total.shape[0], SUB_ROWS):
            here = pl.ds(first, SUB_ROWS)
            held, r1 = total[here, :], scale[here, :]
            rows = normed[here, :].astype(F32)
            inner = jnp.mean(held * rows, axis=1, keepdims=True)
            total[here, :] = r1 * (gain[0:1, :] * held - rows / gain[0:1, :] * inner)
        write_slabs(state, outs, lambda columns: total[:, columns])


def project_back(
    line, gradients, backs, chunk, weight, lead, gains, normed, scale, slabs, mode, after
):
    rows, full = normed.shape
    width = gradients.shape[2]
    rank = lead.shape[2]
    shapes, out_specs = slab_outs(mode, slabs, rows, full // slabs)
    return line.call(
        project_back_kernel,
        "project_back",
        (3,),
        (gradients, backs, weight, lead, gains, normed, scale),
        [
            pl.BlockSpec((1, rows, width), lambda j, s: (j, chunk, 0)),
            pl.BlockSpec((1, rows, rank), lambda j, s: (j, chunk, 0)),
            pl.BlockSpec((1, full, width), lambda j, s: (j, 0, 0)),
            pl.BlockSpec((1, 1, rank, full), lambda j, s: (j, s[1], 0, 0)),
            whole(gains),
            whole(normed),
            whole(scale),
        ],
        shapes,
        out_specs,
        [pltpu.VMEM((rows, full), F32)],
        after,
    )


def rope_tables(length):
    half = HEAD_DIM // 2
    frequency = ROPE_BASE ** (-jnp.arange(half, dtype=F32) * (2.0 / HEAD_DIM))
    angles = jnp.arange(length, dtype=F32)[:, None] * frequency[None, :]
    cosine, sine = jnp.cos(angles), jnp.sin(angles)
    return (
        jnp.concatenate([cosine] * 4, axis=1),
        jnp.concatenate([-sine, sine] * 2, axis=1),
    )


def wire_kernel(n_shared, state, *refs):
    shared_terms, refs = refs[:n_shared], refs[n_shared:]
    split_terms, refs = refs[:6], refs[6:]
    (far, beside, own, split, shared) = refs
    at = 0
    for terms in (shared_terms[0:1], shared_terms[1:3], shared_terms[3:5], shared_terms[5:7]):
        total = terms[0][...]
        for term in terms[1:]:
            total += term[...]
        total = total.astype(BF16).reshape(-1, total.shape[-1])
        shared[at : at + total.shape[0], :] = total
        at += total.shape[0]
    write_slabs(state, (far, beside, own), lambda columns: shared[:, columns])
    unit0, unit1, down0, down1, head, merges = *split_terms[:5], split_terms[5]
    rank, width = head.shape[1:]
    for j in range(2):
        split[j * rank : (j + 1) * rank, :] = (unit0[j] + unit1[j]).astype(BF16)
    split[2 * rank : 3 * rank, :] = (down0[...] + down1[...]).astype(BF16)
    for j in range(3):
        split[3 * rank : 4 * rank, j * width : (j + 1) * width] = head[j].astype(BF16)
    split[3 * rank : 4 * rank, 3 * width :] = (merges[0] + merges[1]).astype(BF16)
    picked = jnp.full((rank, split.shape[1]), state[1].astype(F32))
    split[4 * rank :, :] = picked.astype(BF16)


def own_kernel(state, own, beside, near, far, total):
    held = own[...].astype(F32) + beside[...].astype(F32)
    total[...] = (held + near[...].astype(F32) + far[...].astype(F32)).astype(BF16)


def join_kernel(n_parts, state, *refs):
    parts, (split, joined, shared, sems) = refs[:n_parts], refs[n_parts:]
    copies = slab_copies(state, parts, shared, sems)
    start_copies(copies)
    wait_copies(copies)
    rows = shared.shape[0]
    joined[:rows, :] = shared[...]
    joined[rows:, :] = split[...]


def combine_kernel(
    adapters, width, state, everyone, picks, lead, tail, unit, down, head, merge, slots, held
):
    step = pl.program_id(0)
    count = everyone.shape[0]

    @pl.when(step == 0)
    def _():
        for d in range(count):
            slots[d] = jnp.max(picks[d].astype(F32)).astype(jnp.int32)

    def add_into(target):
        for a in range(adapters):
            target[a] = jnp.zeros(target.shape[1:], F32)
        for d in range(count):
            target[slots[d]] += everyone[d].astype(F32)

    def write(first, blocks, target):
        @pl.when((step >= first) & (step < first + blocks))
        def _():
            add_into(target.at[0])

    write(0, 5, lead)
    write(5, 2, tail)
    write(7, 2, unit)
    write(9, 1, down)

    @pl.when(step == 10)
    def _():
        add_into(held)
        for a in range(adapters):
            for j in range(3):
                head[j, a] = held[a, :, j * width : (j + 1) * width]
            merge[a] = held[a, :, 3 * width :]


class AdapterSums:
    def __init__(self, line, shared, split, slabs):
        rank, full = shared[0].shape[1:]
        width = full // slabs
        self.line, self.rank, self.full, self.width = line, rank, full, width
        slab = (7 * rank, width)
        shapes = ((2, *slab), slab, slab, (5 * rank, full))
        arrays = (*shared, *split)
        far, beside, self.own, self.split = line.call(
            functools.partial(wire_kernel, len(shared)),
            "wire",
            (1,),
            arrays,
            [whole(x) for x in arrays],
            tuple(jax.ShapeDtypeStruct(shape, BF16) for shape in shapes),
            tuple(out_whole(shape) for shape in shapes),
            [pltpu.VMEM((7 * rank, full), BF16)],
        )
        self.slab_sum = SlabSum(line, (far, beside, self.own))

    def cross(self):
        self.slab_sum.cross()

    def spread(self):
        terms = self.slab_sum.terms
        own = self.line.call(
            own_kernel,
            "own",
            (1,),
            terms,
            [whole(x) for x in terms],
            jax.ShapeDtypeStruct(self.own.shape, BF16),
            out_whole(self.own.shape),
        )
        self.parts = spread(own, "pair")

    def join(self):
        shape = (12 * self.rank, self.full)
        sent = self.line.call(
            functools.partial(join_kernel, len(self.parts)),
            "join",
            (1,),
            (*self.parts, self.split),
            [ANY] * len(self.parts) + [whole(self.split)],
            jax.ShapeDtypeStruct(shape, BF16),
            out_whole(shape),
            [pltpu.VMEM((7 * self.rank, self.full), BF16), pltpu.SemaphoreType.DMA((4,))],
        )
        self.everyone = lax.all_gather(sent, "dp", axis=0, tiled=False)

    def combine(self, adapters):
        count = self.everyone.shape[0]
        rank, full, width = self.rank, self.full, self.width

        def sums(first, blocks):
            return pl.BlockSpec(
                (1, adapters, rank, full),
                lambda i, s: (jnp.clip(i - first, 0, blocks - 1), 0, 0, 0),
            )

        def shape(*dims):
            return jax.ShapeDtypeStruct(dims, F32)

        return self.line.call(
            functools.partial(combine_kernel, adapters, width),
            "combine",
            (11,),
            (self.everyone, self.everyone),
            [
                pl.BlockSpec((count, rank, full), lambda i, s: (0, i, 0)),
                pl.BlockSpec((count, rank, 128), lambda i, s: (0, 11, 0)),
            ],
            (
                shape(5, adapters, rank, full),
                shape(2, adapters, rank, full),
                shape(2, adapters, rank, full),
                shape(1, adapters, rank, full),
                shape(3, adapters, rank, width),
                shape(adapters, rank, width),
            ),
            (
                sums(0, 5),
                pl.BlockSpec(
                    (1, adapters, rank, full), lambda i, s: (jnp.where(i < 6, 1, 0), 0, 0, 0)
                ),
                sums(7, 2),
                sums(9, 1),
                out_whole((3, adapters, rank, width)),
                out_whole((adapters, rank, width)),
            ),
            [pltpu.SMEM((count,), jnp.int32), pltpu.VMEM((adapters, rank, full), F32)],
        )


def on_device(
    slabs,
    tokens,
    cotangent,
    norm_gains,
    query_key_value_matrix,
    output_matrix,
    gate_up_matrix,
    down_matrix,
    lead_factors,
    head_factors,
    unit_factors,
    merge_factors,
    down_factors,
    tail_factors,
    doc_ids,
    keep_mask,
    adapter_pick,
):
    length = tokens.shape[1]
    rows = length // CHUNKS
    chosen = adapter_pick[0, 0]
    state = jnp.stack([lax.axis_index("tensor").astype(jnp.int32), chosen])
    line = Line(state)
    gains = norm_gains.astype(F32)
    lead = jnp.swapaxes(lead_factors, 2, 3)
    merge = jnp.swapaxes(merge_factors, 1, 2)
    down = jnp.swapaxes(down_factors, 1, 2)
    cosine, sine = rope_tables(length)
    doc_column = doc_ids.reshape(length, 1)

    def cut(array, c):
        return array[c * rows : (c + 1) * rows]

    own_tokens = [cut(tokens[0], c) for c in range(CHUNKS)]
    token_parts = spread(tokens[0], MODES["tok"])
    own_cots = [cut(cotangent[0], c) for c in range(CHUNKS)]
    cot_parts = spread(cotangent[0], MODES["cot"])

    def project_chunk(c, after=()):
        return project(
            line,
            token_parts,
            c,
            gains,
            lead,
            query_key_value_matrix,
            head_factors,
            cut(cosine, c),
            cut(sine, c),
            after,
        )

    def attend_chunk(c, qkvs, after=()):
        return attend(
            line,
            qkvs,
            c,
            doc_column,
            doc_ids,
            keep_mask,
            output_matrix,
            merge,
            tail_factors,
            slabs,
            MODES["branch"][c],
            after,
        )

    def feed_chunk(c, parts, after=()):
        return feed_forward(
            line,
            parts,
            cot_parts,
            c,
            gains,
            lead,
            gate_up_matrix,
            down_matrix,
            unit_factors,
            down,
            tail_factors,
            (MODES["feed"][c], MODES["back"][c]),
            after,
        )

    def attend_back_chunk(c, parts, after=()):
        return attend_back(
            line,
            parts,
            qkvs[: c + 1],
            c,
            doc_column,
            doc_ids,
            keep_mask,
            attended[c],
            output_matrix,
            merge,
            tail_factors,
            after,
        )

    def project_back_chunk(c, after=()):
        normed, _, scale = saved[c]
        return project_back(
            line,
            gradients,
            backs,
            c,
            query_key_value_matrix,
            lead,
            gains,
            normed,
            scale,
            slabs,
            MODES["last"][c],
            after,
        )

    adapters = lead_factors.shape[1]
    qkv0, *saved0 = project_chunk(0)
    attended0, *branch0 = attend_chunk(0, [qkv0])
    branch0 = SlabSum(line, branch0)
    qkv1, *saved1 = project_chunk(1)
    qkvs, saved = [qkv0, qkv1], [saved0, saved1]
    branch0.cross()
    attended1, *branch1 = attend_chunk(1, qkvs)
    attended = [attended0, attended1]
    branch1 = SlabSum(line, branch1)
    hidden0, rounded0 = branch0.finish(own_tokens[0])
    hidden_parts0 = spread(rounded0, MODES["hidden"][0])
    branch1.cross()
    hidden1, rounded1 = branch1.finish(own_tokens[1])
    hidden_parts1 = spread(rounded1, MODES["hidden"][1])
    feed0, back0, unit_grads0 = feed_chunk(0, hidden_parts0)
    back0 = SlabSum(line, back0)
    feed0 = SlabSum(line, feed0)
    feed1, back1, unit_grads1 = feed_chunk(1, hidden_parts1)
    back1 = SlabSum(line, back1)
    grad0, rounded0 = back0.finish(own_cots[0], (feed0.received,))
    grad_parts0 = spread(rounded0, MODES["grad"][0])
    back1.cross()
    grad1, rounded1 = back1.finish(own_cots[1])
    grad_parts1 = spread(rounded1, MODES["grad"][1])
    query_grad0, key_grad0, value_grad0, *merge_grads0 = attend_back_chunk(0, grad_parts0)
    feed0.cross()
    feed1 = SlabSum(line, relay(line, feed1, (grad_parts1[0],)))
    query_grad1, key_grad1, value_grad1, *merge_grads1 = attend_back_chunk(1, grad_parts1)
    gradients, backs, head_grad, lead_grad = head_back(
        line,
        (query_grad0, query_grad1),
        (key_grad0, key_grad1),
        (value_grad0, value_grad1),
        saved,
        head_factors,
        cosine,
        sine,
    )
    sums = AdapterSums(
        line,
        (
            lead_grad,
            unit_grads0[2],
            unit_grads1[2],
            unit_grads0[3],
            unit_grads1[3],
            merge_grads0[1],
            merge_grads1[1],
        ),
        (
            unit_grads0[0],
            unit_grads1[0],
            unit_grads0[1],
            unit_grads1[1],
            head_grad,
            jnp.stack([merge_grads0[0], merge_grads1[0]]),
        ),
        slabs,
    )
    sums.cross()
    sums.spread()
    last1 = SlabSum(line, project_back_chunk(1, tuple(feed1.terms)))
    sums.join()
    last0 = SlabSum(line, project_back_chunk(0))
    last1.cross()
    last0.cross()
    lead_all, tail_all, unit_all, down_all, head_all, merge_all = sums.combine(adapters)
    _, out0 = feed0.finish(hidden0)
    layer_out = feed1.finish_beside(hidden1, out0, 1)
    _, tokens_grad1 = last1.finish(grad1)
    tokens_grad = last0.finish_beside(grad0, tokens_grad1, 0)
    return (
        layer_out[None],
        tokens_grad[None],
        jnp.swapaxes(lead_all, 2, 3),
        head_all,
        unit_all,
        jnp.swapaxes(merge_all, 1, 2),
        jnp.swapaxes(down_all[0], 1, 2),
        tail_all,
    )


def solution(mesh):
    return jax.shard_map(
        functools.partial(on_device, mesh.shape["tensor"]),
        mesh=mesh,
        in_specs=(
            P("dp", None, "tensor"),
            P("dp", None, "tensor"),
            P(),
            P(None, None, "tensor"),
            P("tensor", None),
            P(None, None, "tensor"),
            P("tensor", None),
            P(),
            P(None, None, None, "tensor"),
            P(None, None, None, "tensor"),
            P(None, "tensor", None),
            P(None, "tensor", None),
            P(),
            P("dp", None),
            P("dp", None),
            P("dp", None),
        ),
        out_specs=(
            P("dp", None, "tensor"),
            P("dp", None, "tensor"),
            P(),
            P(None, None, None, "tensor"),
            P(None, None, None, "tensor"),
            P(None, "tensor", None),
            P(None, "tensor", None),
            P(),
        ),
        check_vma=False,
    )
```

```python
import functools
import math

import jax
import jax.numpy as jnp
from jax import lax
from jax.experimental import pallas as pl
from jax.experimental.pallas import tpu as pltpu
from jax.sharding import PartitionSpec as P

HEAD_DIM = 64
EPSILON = 1e-05
ROPE_BASE = 130000.0
SCALING = 2.0
MASKED = -1000000000.0
LONGEST_DOC = 512
CHUNKS = 2
MODES = {
    "tok": "stack",
    "cot": "stack",
    "branch": ("pair", "pair"),
    "hidden": ("stack", "stack"),
    "feed": ("pair", "stack"),
    "back": ("stack", "pair"),
    "grad": ("stack", "stack"),
    "last": ("pair", "pair"),
}
SUB_ROWS = 256
LARGE_VMEM = 60 * 1024 * 1024
SMALL_VMEM = 30 * 1024 * 1024
LARGE = ("feed_forward", "attend_back", "project_back")

BESIDE = [(0, 1), (1, 0), (2, 3), (3, 2)]
MIDDLE = [(1, 2), (2, 1)]
OVER = [(0, 2), (3, 1)]
ACROSS = [(1, 3), (2, 0)]
OUTWARD = [(1, 0), (2, 3)]
INWARD = [(0, 1), (3, 2)]

F32 = jnp.float32
BF16 = jnp.bfloat16


def dot(a, b):
    return jnp.dot(a, b, preferred_element_type=F32)


def dot_nt(a, b):
    return lax.dot_general(a, b, (((1,), (1,)), ((), ())), preferred_element_type=F32)


def dot_tn(a, b):
    return lax.dot_general(a, b, (((0,), (0,)), ((), ())), preferred_element_type=F32)


def whole(array):
    rank = len(array.shape)
    return pl.BlockSpec(array.shape, lambda *_: (0,) * rank, pipeline_mode=pl.Buffered(1))


ANY = pl.BlockSpec(memory_space=pl.ANY)


def out_whole(shape):
    rank = len(shape)
    return pl.BlockSpec(shape, lambda *_: (0,) * rank)


def spread(own, mode):
    if mode == "stack":
        return [lax.all_gather(own, "tensor", axis=0, tiled=False)]
    beside = lax.ppermute(own, "tensor", BESIDE)
    near = lax.ppermute(own, "tensor", MIDDLE)
    far = lax.ppermute(own, "tensor", OVER)
    return [
        own,
        beside,
        near,
        far,
        lax.ppermute(near, "tensor", OUTWARD),
        lax.ppermute(far, "tensor", OUTWARD),
    ]


def slab_columns(slab, width):
    return pl.ds(pl.multiple_of(slab * width, width), width)


def slab_copies(state, parts, target, sems, first=0):
    here = pl.ds(first, target.shape[0])
    width = parts[0].shape[-1]
    if len(parts) == 1:
        return [
            (None, pltpu.make_async_copy(
                parts[0].at[j, here], target.at[:, j * width : (j + 1) * width], sems.at[j]
            ))
            for j in range(parts[0].shape[0])
        ]
    me, inner, near, far = places(state)
    copies = []
    for sem, (condition, part, slab) in enumerate((
        (None, parts[0], me),
        (None, parts[1], beside_of(me)),
        (inner, parts[2], near),
        (inner, parts[3], far),
        (jnp.logical_not(inner), parts[4], near),
        (jnp.logical_not(inner), parts[5], far),
    )):
        copies.append((condition, pltpu.make_async_copy(
            part.at[here], target.at[:, slab_columns(slab, width)], sems.at[sem % 4 + 2 * (sem // 4)]
        )))
    return copies


def beside_of(me):
    return me + 1 - 2 * lax.rem(me, 2)


def places(state):
    me = state[0]
    upper = me >= 2
    return me, (me == 1) | (me == 2), jnp.where(upper, 1, 2), jnp.where(upper, 0, 3)


def each_copy(copies, act):
    for condition, copy in copies:
        if condition is None:
            act(copy)
        else:
            pl.when(condition)(functools.partial(act, copy))


def start_copies(copies):
    each_copy(copies, lambda copy: copy.start())


def wait_copies(copies):
    each_copy(copies, lambda copy: copy.wait())


def write_slabs(state, outs, term):
    width = outs[0].shape[-1]
    if len(outs) == 1:
        for slab in range(outs[0].shape[0]):
            outs[0][slab] = term(slab_columns(slab, width)).astype(BF16)
        return
    me, _, near, far = places(state)
    for target, slab in (
        (outs[0].at[0], near),
        (outs[0].at[1], far),
        (outs[1], beside_of(me)),
        (outs[2], me),
    ):
        target[...] = term(slab_columns(slab, width)).astype(BF16)


def slab_outs(mode, count, rows, width):
    if mode == "stack":
        shapes = ((count, rows, width),)
    else:
        shapes = ((2, rows, width), (rows, width), (rows, width))
    return (
        tuple(jax.ShapeDtypeStruct(shape, BF16) for shape in shapes),
        tuple(out_whole(shape) for shape in shapes),
    )


def add_kernel(state, far, received, beside, near_out, far_out, beside_out):
    near_out[...] = (far[0].astype(F32) + received[0].astype(F32)).astype(BF16)
    far_out[...] = (far[1].astype(F32) + received[1].astype(F32)).astype(BF16)
    beside_out[...] = beside[...]


def sum_kernel(state, *refs):
    terms, (exact, rounded) = refs[:-2], refs[-2:]
    total = terms[0][...].astype(F32)
    for term in terms[1:]:
        total += term[...].astype(F32)
    exact[...] = total
    rounded[...] = total.astype(BF16)


def sum_beside_kernel(chunk, count, state, other, *refs):
    terms, joined = refs[:-1], refs[-1]
    here = pl.program_id(0) // count == chunk

    @pl.when(jnp.logical_not(here))
    def _():
        joined[...] = other[...]

    @pl.when(here)
    def _():
        total = terms[0][...].astype(F32)
        for term in terms[1:]:
            total += term[...].astype(F32)
        joined[...] = total.astype(BF16)


def relay_kernel(state, *refs):
    count = len(refs) // 2
    for source, target in zip(refs[:count], refs[count:]):
        target[...] = source[...]


def relay(line, parts, after=()):
    return line.call(
        relay_kernel,
        "relay",
        (1,),
        parts,
        [whole(x) for x in parts],
        tuple(jax.ShapeDtypeStruct(x.shape, x.dtype) for x in parts),
        tuple(out_whole(x.shape) for x in parts),
        after=after,
    )


class SlabSum:
    def __init__(self, line, parts):
        self.line, self.parts = line, parts
        if len(parts) == 1:
            self.terms = [
                lax.psum_scatter(parts[0], "tensor", scatter_dimension=0, tiled=False)
            ]
        else:
            self.received = lax.ppermute(parts[0], "tensor", INWARD)

    def cross(self, after=()):
        far, beside, own = self.parts
        rows, width = own.shape
        step = min(256, rows)
        flat = pl.BlockSpec((step, width), lambda i, s: (i, 0))
        both = pl.BlockSpec((2, step, width), lambda i, s: (0, i, 0))
        near, far, beside = self.line.call(
            add_kernel,
            "add",
            (rows // step,),
            (far, self.received, beside),
            [both, both, flat],
            (jax.ShapeDtypeStruct((rows, width), BF16),) * 3,
            (flat,) * 3,
            after=after,
        )
        near = lax.ppermute(near, "tensor", MIDDLE)
        far = lax.ppermute(far, "tensor", ACROSS)
        beside = lax.ppermute(beside, "tensor", BESIDE)
        self.terms = [own, beside, near, far]

    def finish(self, base, after=()):
        rows, width = base.shape
        step = min(256, rows)
        flat = pl.BlockSpec((step, width), lambda i, s: (i, 0))
        return self.line.call(
            sum_kernel,
            "sum",
            (rows // step,),
            (base, *self.terms),
            [flat] * (1 + len(self.terms)),
            (jax.ShapeDtypeStruct((rows, width), F32), jax.ShapeDtypeStruct((rows, width), BF16)),
            (flat, flat),
            after=after,
        )


    def finish_beside(self, base, other, chunk):
        rows, width = base.shape
        step = min(256, rows)
        count = rows // step

        def rows_of(c):
            return pl.BlockSpec(
                (step, width), lambda i, s: (jnp.clip(i - c * count, 0, count - 1), 0)
            )

        return self.line.call(
            functools.partial(sum_beside_kernel, chunk, count),
            "sum_beside",
            (2 * count,),
            (other, base, *self.terms),
            [rows_of(1 - chunk)] + [rows_of(chunk)] * (1 + len(self.terms)),
            jax.ShapeDtypeStruct((2 * rows, width), BF16),
            pl.BlockSpec((step, width), lambda i, s: (i, 0)),
        )


def params(name):
    return pltpu.CompilerParams(
        dimension_semantics=("arbitrary",),
        vmem_limit_bytes=LARGE_VMEM if name in LARGE else SMALL_VMEM,
    )


class Line:
    def __init__(self, state):
        self.state, self.last = state, ()

    def call(self, kernel, name, grid, ins, in_specs, outs, out_specs, scratch=(), after=()):
        after = (*self.last, *after)
        n_used = 1 + len(ins)

        def body(*refs):
            kernel(*refs[:n_used], *refs[n_used + len(after) :])

        results = pl.pallas_call(
            body,
            name=name,
            grid_spec=pltpu.PrefetchScalarGridSpec(
                num_scalar_prefetch=1,
                grid=grid,
                in_specs=list(in_specs) + [ANY] * len(after),
                out_specs=out_specs,
                scratch_shapes=list(scratch),
            ),
            out_shape=outs,
            compiler_params=params(name),
            cost_estimate=pl.CostEstimate(flops=1, bytes_accessed=1, transcendentals=0),
        )(self.state, *ins, *after)
        self.last = (jax.tree.leaves(results)[-1],)
        return results


def swap_halves(values):
    width = values.shape[-1]
    half = HEAD_DIM // 2
    lane = lax.broadcasted_iota(jnp.int32, values.shape, values.ndim - 1) % HEAD_DIM
    return jnp.where(
        lane < half,
        pltpu.roll(values, width - half, values.ndim - 1),
        pltpu.roll(values, half, values.ndim - 1),
    )


def rope_groups(values, cosine, sine, sign):
    groups = []
    for first in range(0, values.shape[-1], 128):
        group = values[:, first : first + 128]
        groups.append(group * cosine + (sign * swap_halves(group)) * sine)
    return jnp.concatenate(groups, axis=-1)


def project_kernel(first_row, n_parts, state, *refs):
    parts, refs = refs[:n_parts], refs[n_parts:]
    gain, lead, weight, head, cosine, sine, qkv, normed, mid, scale, stream, sems = refs
    step = pl.program_id(0)
    rank = lead.shape[2]

    @pl.when(step == 0)
    def _():
        copies = slab_copies(state, parts, stream, sems, first_row)
        start_copies(copies)
        wait_copies(copies)
        for first in range(0, stream.shape[0], SUB_ROWS):
            here = pl.ds(first, SUB_ROWS)
            rows = stream[here, :].astype(F32)
            r1 = lax.rsqrt(jnp.mean(rows * rows, axis=1, keepdims=True) + EPSILON)
            scale[here, :] = r1
            values = (rows * r1 * gain[0:1, :]).astype(BF16)
            normed[here, :] = values
            mids = dot_nt(values, lead[:3, 0].reshape(3 * rank, -1))
            for j in range(3):
                mid[j, here, :] = mids[:, j * rank : (j + 1) * rank].astype(BF16)

    for first in range(0, stream.shape[0], SUB_ROWS):
        here = pl.ds(first, SUB_ROWS)
        projected = dot(normed[here, :], weight[0]) + SCALING * dot(mid[step, here, :], head[0, 0])

        @pl.when(step < 2)
        def _():
            qkv[0, here, :] = rope_groups(projected, cosine[here, :], sine[here, :], 1.0).astype(BF16)

        @pl.when(step == 2)
        def _():
            qkv[0, here, :] = projected.astype(BF16)


def project(line, parts, chunk, gains, lead, weight, head, cosine, sine, after=()):
    rows = cosine.shape[0]
    full, width = weight.shape[1:]
    rank = lead.shape[2]
    slabs = full // parts[0].shape[-1]
    return line.call(
        functools.partial(project_kernel, chunk * rows, len(parts)),
        "project",
        (3,),
        (*parts, gains, lead, weight, head, cosine, sine),
        [ANY] * len(parts)
        + [
            whole(gains),
            pl.BlockSpec(
                (lead.shape[0], 1, rank, full),
                lambda j, s: (0, s[1], 0, 0),
                pipeline_mode=pl.Buffered(1),
            ),
            pl.BlockSpec((1, full, width), lambda j, s: (j, 0, 0)),
            pl.BlockSpec((1, 1, rank, width), lambda j, s: (j, s[1], 0, 0)),
            whole(cosine),
            whole(sine),
        ],
        (
            jax.ShapeDtypeStruct((3, rows, width), BF16),
            jax.ShapeDtypeStruct((rows, full), BF16),
            jax.ShapeDtypeStruct((3, rows, rank), BF16),
            jax.ShapeDtypeStruct((rows, 1), F32),
        ),
        (
            pl.BlockSpec((1, rows, width), lambda j, s: (j, 0, 0)),
            out_whole((rows, full)),
            out_whole((3, rows, rank)),
            out_whole((rows, 1)),
        ),
        [pltpu.VMEM((rows, full), BF16), pltpu.SemaphoreType.DMA((slabs,))],
        after,
    )


def head_mask(shape, half):
    lane = lax.broadcasted_iota(jnp.int32, shape, len(shape) - 1)
    return (lane >= HEAD_DIM) if half else (lane < HEAD_DIM)


def key_span(first_row, block):
    low = max(0, first_row - LONGEST_DOC + 1)
    return (low // 128) * 128, first_row + block


def key_bias(doc_rows, doc_keys, keep_keys, first_row, low, high, block):
    rows_at = first_row + lax.broadcasted_iota(jnp.int32, (block, high - low), 0)
    keys_at = low + lax.broadcasted_iota(jnp.int32, (block, high - low), 1)
    same = doc_rows == doc_keys[:, low:high]
    live = (keep_keys[:, low:high] == 1) | (rows_at == keys_at)
    return jnp.where((keys_at <= rows_at) & same & live, 0.0, MASKED)


def attend_kernel(first_row, block, n_chunks, n_outs, state, *refs):
    chunks, refs = refs[: 2 * n_chunks], refs[2 * n_chunks :]
    query, doc_rows, doc_keys, keep, weight, merge, tail = refs[:7]
    attended, refs = refs[7], refs[8:]
    branch, (keys, values, bias, held) = refs[:n_outs], refs[n_outs:]
    step = pl.program_id(0)
    rows = query.shape[1]
    for c in range(n_chunks):
        keys[c * rows : (c + 1) * rows, :] = chunks[2 * c][0]
        values[c * rows : (c + 1) * rows, :] = chunks[2 * c + 1][0]
    for sub in range(rows // block):
        start = first_row + sub * block
        low, high = key_span(start, block)
        here = pl.ds(sub * block, block)

        @pl.when(step == 0)
        def _():
            bias[sub, :, : high - low] = key_bias(
                doc_rows[here, :], doc_keys[...], keep[...], start, low, high, block
            )

        outs = []
        for half in range(2):
            mask = head_mask((block, 128), half)
            q = jnp.where(mask, query[0, here, :] * (HEAD_DIM**-0.5), 0.0).astype(BF16)
            scores = dot_nt(q, keys[low:high, :]) + bias[sub, :, : high - low]
            raised = jnp.exp(scores - jnp.max(scores, axis=1, keepdims=True))
            total = jnp.sum(raised, axis=1, keepdims=True)
            weights = (raised * (1.0 / total)).astype(BF16)
            outs.append(dot(weights, values[low:high, :]))
        columns = pl.ds(pl.multiple_of(step * 128, 128), 128)
        held[here, columns] = jnp.where(head_mask((block, 128), 0), outs[0], outs[1]).astype(BF16)

    @pl.when(step == pl.num_programs(0) - 1)
    def _():
        result = held[...]
        attended[...] = result
        mid = dot_nt(result, merge[0]).astype(BF16)
        write_slabs(
            state,
            branch,
            lambda columns: dot(result, weight[:, columns])
            + SCALING * dot(mid, tail[0, 0, :, columns]),
        )


def attend(line, qkvs, chunk, doc_column, doc_row, keep_row, weight, merge, tail, slabs, mode, after=()):
    rows, width = qkvs[0].shape[1:]
    first_row = chunk * rows
    block = min(256, rows)
    n_chunks = chunk + 1
    rank, full = merge.shape[1], weight.shape[1]
    ins, specs = [], []
    for c in range(n_chunks):
        for j in (1, 2):
            ins.append(qkvs[c])
            specs.append(pl.BlockSpec((1, rows, 128), lambda i, s, j=j: (j, 0, i)))
    ins += [qkvs[chunk], doc_column, doc_row, keep_row, weight, merge, tail]
    specs += [
        pl.BlockSpec((1, rows, 128), lambda i, s: (0, 0, i)),
        pl.BlockSpec((rows, 1), lambda i, s: (chunk, 0), pipeline_mode=pl.Buffered(1)),
        whole(doc_row),
        whole(keep_row),
        whole(weight),
        pl.BlockSpec((1, rank, width), lambda i, s: (s[1], 0, 0), pipeline_mode=pl.Buffered(1)),
        pl.BlockSpec(
            (1, 1, rank, full), lambda i, s: (0, s[1], 0, 0), pipeline_mode=pl.Buffered(1)
        ),
    ]
    n_keys = first_row + rows
    shapes, out_specs = slab_outs(mode, slabs, rows, full // slabs)
    outs = line.call(
        functools.partial(attend_kernel, first_row, block, n_chunks, len(shapes)),
        "attend",
        (width // 128,),
        ins,
        specs,
        (jax.ShapeDtypeStruct((rows, width), BF16),) + shapes,
        (out_whole((rows, width)),) + out_specs,
        [
            pltpu.VMEM((n_keys, 128), BF16),
            pltpu.VMEM((n_keys, 128), BF16),
            pltpu.VMEM((rows // block, block, min(n_keys, LONGEST_DOC + block)), F32),
            pltpu.VMEM((rows, width), BF16),
        ],
        after,
    )
    return outs


def feed_kernel(first_row, n_parts, n_cots, n_feed, n_back, state, *refs):
    parts, refs = refs[:n_parts], refs[n_parts:]
    cot_parts, refs = refs[:n_cots], refs[n_cots:]
    gain, lead, gate_w, up_w, down_w, unit, down, tail = refs[:8]
    refs = refs[8:]
    feed, refs = refs[:n_feed], refs[n_feed:]
    back, refs = refs[:n_back], refs[n_back:]
    unit_grad, down_grad, lead_grad, tail_grad = refs[:4]
    stream, upstream, normed, mid, down_back, scale = refs[4:10]
    feed_sum, back_sum, down_mid, unit_back, sems, cot_sems = refs[10:]
    step = pl.program_id(0)
    rank = lead.shape[2]
    firsts = range(0, stream.shape[0], SUB_ROWS)

    @pl.when(step == 0)
    def _():
        copies = slab_copies(state, parts, stream, sems)
        cot_copies = slab_copies(state, cot_parts, upstream, cot_sems, first_row)
        start_copies(copies)
        start_copies(cot_copies)
        wait_copies(copies)
        for first in firsts:
            here = pl.ds(first, SUB_ROWS)
            rows = stream[here, :].astype(F32)
            r2 = lax.rsqrt(jnp.mean(rows * rows, axis=1, keepdims=True) + EPSILON)
            scale[here, :] = r2
            values = (rows * r2 * gain[1:2, :]).astype(BF16)
            normed[here, :] = values
            mids = dot_nt(values, lead[3:5, 0].reshape(2 * rank, -1))
            for j in range(2):
                mid[j, here, :] = mids[:, j * rank : (j + 1) * rank].astype(BF16)
        wait_copies(cot_copies)
        down_back[...] = (SCALING * dot_nt(upstream[...], tail[0, 0])).astype(BF16)
        feed_sum[...] = jnp.zeros_like(feed_sum)
        back_sum[...] = jnp.zeros_like(back_sum)
        down_mid[...] = jnp.zeros_like(down_mid)
        unit_back[...] = jnp.zeros_like(unit_back)

    unit_terms = [0.0, 0.0]
    down_term = 0.0
    for first in firsts:
        here = pl.ds(first, SUB_ROWS)
        gate = dot(normed[here, :], gate_w[0]) + SCALING * dot(mid[0, here, :], unit[0, 0])
        up = dot(normed[here, :], up_w[0]) + SCALING * dot(mid[1, here, :], unit[1, 0])
        hidden_grad = dot_nt(upstream[here, :], down_w[...]) + dot(down_back[here, :], down[0])
        sigma = 1.0 / (1.0 + jnp.exp(-gate))
        active = gate * sigma
        hidden = (active * up).astype(BF16)
        up_grad = (hidden_grad * active).astype(BF16)
        gate_grad = (hidden_grad * up * (sigma + active * (1.0 - sigma))).astype(BF16)
        feed_sum[here, :] += dot(hidden, down_w[...])
        back_sum[here, :] += dot_nt(gate_grad, gate_w[0]) + dot_nt(up_grad, up_w[0])
        down_mid[here, :] += dot_nt(hidden, down[0])
        unit_back[0, here, :] += dot_nt(gate_grad, unit[0, 0])
        unit_back[1, here, :] += dot_nt(up_grad, unit[1, 0])
        unit_terms[0] += dot_tn(mid[0, here, :], gate_grad)
        unit_terms[1] += dot_tn(mid[1, here, :], up_grad)
        down_term += dot_tn(down_back[here, :], hidden)
    unit_grad[0] = SCALING * unit_terms[0]
    unit_grad[1] = SCALING * unit_terms[1]
    down_grad[...] = down_term

    @pl.when(step == pl.num_programs(0) - 1)
    def _():
        values = normed[...]
        mid_down = down_mid[...].astype(BF16)
        tail_grad[...] = SCALING * dot_tn(mid_down, upstream[...])
        unit_backs = [(SCALING * unit_back[j]).astype(BF16) for j in range(2)]
        for j in range(2):
            lead_grad[j] = dot_tn(unit_backs[j], values)
        write_slabs(
            state,
            feed,
            lambda columns: feed_sum[:, columns] + SCALING * dot(mid_down, tail[0, 0, :, columns]),
        )
        for first in firsts:
            here = pl.ds(first, SUB_ROWS)
            there = slice(first, first + SUB_ROWS)
            r2 = scale[here, :]
            total = back_sum[here, :]
            for j in range(2):
                total += dot(unit_backs[j][there], lead[3 + j, 0])
            inner = jnp.mean(total * normed[here, :].astype(F32), axis=1, keepdims=True)
            back_sum[here, :] = r2 * (
                gain[1:2, :] * total - stream[here, :].astype(F32) * (r2 * inner)
            )
        write_slabs(state, back, lambda columns: back_sum[:, columns])


def feed_forward(
    line, parts, cot_parts, chunk, gains, lead, gate_up, down_w, unit, down, tail, modes, after=()
):
    feed_mode, back_mode = modes
    rows, slab_width = parts[0].shape[-2:]
    full, units = gate_up.shape[1:]
    rank = lead.shape[2]
    slabs = full // slab_width
    block = min(512, units)
    feed_shapes, feed_specs = slab_outs(feed_mode, slabs, rows, slab_width)
    back_shapes, back_specs = slab_outs(back_mode, slabs, rows, slab_width)
    outs = line.call(
        functools.partial(
            feed_kernel, chunk * rows, len(parts), len(cot_parts), len(feed_shapes), len(back_shapes)
        ),
        "feed_forward",
        (units // block,),
        (*parts, *cot_parts, gains, lead, gate_up, gate_up, down_w, unit, down, tail),
        [ANY] * (len(parts) + len(cot_parts))
        + [
            whole(gains),
            pl.BlockSpec(
                (lead.shape[0], 1, rank, full),
                lambda i, s: (0, s[1], 0, 0),
                pipeline_mode=pl.Buffered(1),
            ),
            pl.BlockSpec((1, full, block), lambda i, s: (0, 0, i)),
            pl.BlockSpec((1, full, block), lambda i, s: (1, 0, i)),
            pl.BlockSpec((block, full), lambda i, s: (i, 0)),
            pl.BlockSpec((2, 1, rank, block), lambda i, s: (0, s[1], 0, i)),
            pl.BlockSpec((1, rank, block), lambda i, s: (s[1], 0, i)),
            pl.BlockSpec(
                (1, 1, rank, full), lambda i, s: (1, s[1], 0, 0), pipeline_mode=pl.Buffered(1)
            ),
        ],
        feed_shapes
        + back_shapes
        + (
            jax.ShapeDtypeStruct((2, rank, units), F32),
            jax.ShapeDtypeStruct((rank, units), F32),
            jax.ShapeDtypeStruct((2, rank, full), F32),
            jax.ShapeDtypeStruct((rank, full), F32),
        ),
        feed_specs
        + back_specs
        + (
            pl.BlockSpec((2, rank, block), lambda i, s: (0, 0, i)),
            pl.BlockSpec((rank, block), lambda i, s: (0, i)),
            out_whole((2, rank, full)),
            out_whole((rank, full)),
        ),
        [
            pltpu.VMEM((rows, full), BF16),
            pltpu.VMEM((rows, full), BF16),
            pltpu.VMEM((rows, full), BF16),
            pltpu.VMEM((2, rows, rank), BF16),
            pltpu.VMEM((rows, rank), BF16),
            pltpu.VMEM((rows, 1), F32),
            pltpu.VMEM((rows, full), F32),
            pltpu.VMEM((rows, full), F32),
            pltpu.VMEM((rows, rank), F32),
            pltpu.VMEM((2, rows, rank), F32),
            pltpu.SemaphoreType.DMA((slabs,)),
            pltpu.SemaphoreType.DMA((slabs,)),
        ],
        after,
    )
    n_feed, n_both = len(feed_shapes), len(feed_shapes) + len(back_shapes)
    return list(outs[:n_feed]), list(outs[n_feed:n_both]), outs[n_both:]


def attend_back_kernel(first_row, block, n_chunks, n_parts, state, *refs):
    parts, refs = refs[:n_parts], refs[n_parts:]
    chunks, refs = refs[: 2 * n_chunks], refs[2 * n_chunks :]
    query, doc_rows, doc_keys, keep, attended, weight, merge, tail = refs[:8]
    query_grad, key_grad, value_grad, merge_grad, tail_grad = refs[8:13]
    keys, values, bias, branch, out_grad, sems = refs[13:]
    step = pl.program_id(0)
    rows = query.shape[1]
    inverse_root = HEAD_DIM**-0.5

    @pl.when(step == 0)
    def _():
        copies = slab_copies(state, parts, branch, sems)
        start_copies(copies)
        wait_copies(copies)
        gradient = branch[...]
        result = attended[...]
        merge_back = (SCALING * dot_nt(gradient, tail[0, 0])).astype(BF16)
        merge_mid = dot_nt(result, merge[0]).astype(BF16)
        merge_grad[...] = dot_tn(merge_back, result)
        tail_grad[...] = SCALING * dot_tn(merge_mid, gradient)
        whole_grad = (dot_nt(gradient, weight[...]) + dot(merge_back, merge[0])).astype(BF16)
        for pair in range(out_grad.shape[0]):
            out_grad[pair] = whole_grad[:, pair * 128 : (pair + 1) * 128]

    for c in range(n_chunks):
        keys[c * rows : (c + 1) * rows, :] = chunks[2 * c][0]
        values[c * rows : (c + 1) * rows, :] = chunks[2 * c + 1][0]
    key_grad[...] = jnp.zeros_like(key_grad)
    value_grad[...] = jnp.zeros_like(value_grad)
    for sub in range(rows // block):
        start = first_row + sub * block
        low, high = key_span(start, block)
        here = pl.ds(sub * block, block)

        @pl.when(step == 0)
        def _():
            bias[sub, :, : high - low] = key_bias(
                doc_rows[here, :], doc_keys[...], keep[...], start, low, high, block
            )

        outs = []
        key_term = value_term = 0.0
        for half in range(2):
            mask = head_mask((block, 128), half)
            q = jnp.where(mask, query[0, here, :] * inverse_root, 0.0).astype(BF16)
            grad = jnp.where(mask, out_grad[step, here, :], 0.0).astype(BF16)
            scores = dot_nt(q, keys[low:high, :]) + bias[sub, :, : high - low]
            raised = jnp.exp(scores - jnp.max(scores, axis=1, keepdims=True))
            probs = raised * (1.0 / jnp.sum(raised, axis=1, keepdims=True))
            prob_grad = dot_nt(grad, values[low:high, :])
            inner = jnp.sum(probs * prob_grad, axis=1, keepdims=True)
            score_grad = (probs * (prob_grad - inner)).astype(BF16)
            outs.append(dot(score_grad, keys[low:high, :]))
            key_term += dot_tn(score_grad, q)
            value_term += dot_tn(probs.astype(BF16), grad)
        mixed = jnp.where(head_mask((block, 128), 0), outs[0], outs[1])
        query_grad[here, :] = mixed * inverse_root
        key_grad[low:high, :] += key_term
        value_grad[low:high, :] += value_term


def attend_back(line, parts, qkvs, chunk, doc_column, doc_row, keep_row, attended, weight, merge, tail, after=()):
    rows, width = qkvs[0].shape[1:]
    first_row = chunk * rows
    block = min(256, rows)
    n_chunks = chunk + 1
    rank, full = merge.shape[1], weight.shape[1]
    slabs = full // parts[0].shape[-1]
    ins, specs = list(parts), [ANY] * len(parts)
    for c in range(n_chunks):
        for j in (1, 2):
            ins.append(qkvs[c])
            specs.append(pl.BlockSpec((1, rows, 128), lambda i, s, j=j: (j, 0, i)))
    ins += [qkvs[chunk], doc_column, doc_row, keep_row, attended, weight, merge, tail]
    specs += [
        pl.BlockSpec((1, rows, 128), lambda i, s: (0, 0, i)),
        pl.BlockSpec((rows, 1), lambda i, s: (chunk, 0), pipeline_mode=pl.Buffered(1)),
        whole(doc_row),
        whole(keep_row),
        whole(attended),
        whole(weight),
        pl.BlockSpec((1, rank, width), lambda i, s: (s[1], 0, 0), pipeline_mode=pl.Buffered(1)),
        pl.BlockSpec(
            (1, 1, rank, full), lambda i, s: (0, s[1], 0, 0), pipeline_mode=pl.Buffered(1)
        ),
    ]
    n_keys = first_row + rows
    return line.call(
        functools.partial(attend_back_kernel, first_row, block, n_chunks, len(parts)),
        "attend_back",
        (width // 128,),
        ins,
        specs,
        (
            jax.ShapeDtypeStruct((rows, width), F32),
            jax.ShapeDtypeStruct((n_keys, width), F32),
            jax.ShapeDtypeStruct((n_keys, width), F32),
            jax.ShapeDtypeStruct((rank, width), F32),
            jax.ShapeDtypeStruct((rank, full), F32),
        ),
        (
            pl.BlockSpec((rows, 128), lambda i, s: (0, i)),
            pl.BlockSpec((n_keys, 128), lambda i, s: (0, i)),
            pl.BlockSpec((n_keys, 128), lambda i, s: (0, i)),
            out_whole((rank, width)),
            out_whole((rank, full)),
        ),
        [
            pltpu.VMEM((n_keys, 128), BF16),
            pltpu.VMEM((n_keys, 128), BF16),
            pltpu.VMEM((rows // block, block, min(n_keys, LONGEST_DOC + block)), F32),
            pltpu.VMEM((rows, full), BF16),
            pltpu.VMEM((width // 128, rows, 128), BF16),
            pltpu.SemaphoreType.DMA((slabs,)),
        ],
        after,
    )


def head_back_kernel(state, *refs):
    query_grads, key_grads, value_grads = refs[0:2], refs[2:4], refs[4:6]
    normed, mids = refs[6:8], refs[8:10]
    head, cosine, sine = refs[10:13]
    gradients, backs, head_grad, lead_grad = refs[13:]
    rows = query_grads[0].shape[0]
    rank = head.shape[2]
    head_terms = [jnp.zeros(head_grad.shape[1:], F32) for _ in range(3)]
    lead_term = jnp.zeros((3 * rank, lead_grad.shape[2]), F32)
    for c in range(2):
        for first in range(0, rows, SUB_ROWS):
            here = pl.ds(first, SUB_ROWS)
            there = pl.ds(c * rows + first, SUB_ROWS)
            key, value = key_grads[1][there, :], value_grads[1][there, :]
            if c == 0:
                key, value = key + key_grads[0][here, :], value + value_grads[0][here, :]
            tables = cosine[there, :], sine[there, :], -1.0
            turned = (
                rope_groups(query_grads[c][here, :], *tables),
                rope_groups(key, *tables),
                value,
            )
            back = []
            for j in range(3):
                gradient = turned[j].astype(BF16)
                gradients[j, there, :] = gradient
                back.append((SCALING * dot_nt(gradient, head[j, 0])).astype(BF16))
                backs[j, there, :] = back[j]
                head_terms[j] += dot_tn(mids[c][j, here, :], gradient)
            lead_term += dot_tn(jnp.concatenate(back, axis=1), normed[c][here, :])
    for j in range(3):
        head_grad[j] = SCALING * head_terms[j]
        lead_grad[j] = lead_term[j * rank : (j + 1) * rank]


def head_back(line, query_grads, key_grads, value_grads, saved, head, cosine, sine):
    rows, width = query_grads[0].shape
    full = saved[0][0].shape[1]
    rank = head.shape[2]
    ins = (
        *query_grads,
        *key_grads,
        *value_grads,
        *(normed for normed, _, _ in saved),
        *(mid for _, mid, _ in saved),
    )
    shapes = (
        ((3, 2 * rows, width), BF16),
        ((3, 2 * rows, rank), BF16),
        ((3, rank, width), F32),
        ((3, rank, full), F32),
    )
    return line.call(
        head_back_kernel,
        "head_back",
        (1,),
        (*ins, head, cosine, sine),
        [whole(x) for x in ins]
        + [
            pl.BlockSpec(
                (3, 1, rank, width), lambda i, s: (0, s[1], 0, 0), pipeline_mode=pl.Buffered(1)
            ),
            whole(cosine),
            whole(sine),
        ],
        tuple(jax.ShapeDtypeStruct(*shape) for shape in shapes),
        tuple(out_whole(shape) for shape, _ in shapes),
    )


def project_back_kernel(state, gradient, back, weight, lead, gain, normed, scale, *refs):
    outs, total = refs[:-1], refs[-1]
    step = pl.program_id(0)
    for first in range(0, total.shape[0], SUB_ROWS):
        here = pl.ds(first, SUB_ROWS)
        term = dot_nt(gradient[0, here, :], weight[0]) + dot(back[0, here, :], lead[0, 0])

        @pl.when(step == 0)
        def _():
            total[here, :] = term

        @pl.when(step > 0)
        def _():
            total[here, :] += term

    @pl.when(step == pl.num_programs(0) - 1)
    def _():
        for first in range(0, total.shape[0], SUB_ROWS):
            here = pl.ds(first, SUB_ROWS)
            held, r1 = total[here, :], scale[here, :]
            rows = normed[here, :].astype(F32)
            inner = jnp.mean(held * rows, axis=1, keepdims=True)
            total[here, :] = r1 * (gain[0:1, :] * held - rows / gain[0:1, :] * inner)
        write_slabs(state, outs, lambda columns: total[:, columns])


def project_back(
    line, gradients, backs, chunk, weight, lead, gains, normed, scale, slabs, mode, after
):
    rows, full = normed.shape
    width = gradients.shape[2]
    rank = lead.shape[2]
    shapes, out_specs = slab_outs(mode, slabs, rows, full // slabs)
    return line.call(
        project_back_kernel,
        "project_back",
        (3,),
        (gradients, backs, weight, lead, gains, normed, scale),
        [
            pl.BlockSpec((1, rows, width), lambda j, s: (j, chunk, 0)),
            pl.BlockSpec((1, rows, rank), lambda j, s: (j, chunk, 0)),
            pl.BlockSpec((1, full, width), lambda j, s: (j, 0, 0)),
            pl.BlockSpec((1, 1, rank, full), lambda j, s: (j, s[1], 0, 0)),
            whole(gains),
            whole(normed),
            whole(scale),
        ],
        shapes,
        out_specs,
        [pltpu.VMEM((rows, full), F32)],
        after,
    )


def rope_tables(length):
    half = HEAD_DIM // 2
    frequency = ROPE_BASE ** (-jnp.arange(half, dtype=F32) * (2.0 / HEAD_DIM))
    angles = jnp.arange(length, dtype=F32)[:, None] * frequency[None, :]
    cosine, sine = jnp.cos(angles), jnp.sin(angles)
    return (
        jnp.concatenate([cosine] * 4, axis=1),
        jnp.concatenate([-sine, sine] * 2, axis=1),
    )


def wire_kernel(n_shared, state, *refs):
    shared_terms, refs = refs[:n_shared], refs[n_shared:]
    split_terms, refs = refs[:6], refs[6:]
    (far, beside, own, split, shared) = refs
    at = 0
    for terms in (shared_terms[0:1], shared_terms[1:3], shared_terms[3:5], shared_terms[5:7]):
        total = terms[0][...]
        for term in terms[1:]:
            total += term[...]
        total = total.astype(BF16).reshape(-1, total.shape[-1])
        shared[at : at + total.shape[0], :] = total
        at += total.shape[0]
    write_slabs(state, (far, beside, own), lambda columns: shared[:, columns])
    unit0, unit1, down0, down1, head, merges = *split_terms[:5], split_terms[5]
    rank, width = head.shape[1:]
    for j in range(2):
        split[j * rank : (j + 1) * rank, :] = (unit0[j] + unit1[j]).astype(BF16)
    split[2 * rank : 3 * rank, :] = (down0[...] + down1[...]).astype(BF16)
    for j in range(3):
        split[3 * rank : 4 * rank, j * width : (j + 1) * width] = head[j].astype(BF16)
    split[3 * rank : 4 * rank, 3 * width :] = (merges[0] + merges[1]).astype(BF16)
    picked = jnp.full((rank, split.shape[1]), state[1].astype(F32))
    split[4 * rank :, :] = picked.astype(BF16)


def own_kernel(state, own, beside, near, far, total):
    held = own[...].astype(F32) + beside[...].astype(F32)
    total[...] = (held + near[...].astype(F32) + far[...].astype(F32)).astype(BF16)


def join_kernel(n_parts, state, *refs):
    parts, (split, joined, shared, sems) = refs[:n_parts], refs[n_parts:]
    copies = slab_copies(state, parts, shared, sems)
    start_copies(copies)
    wait_copies(copies)
    rows = shared.shape[0]
    joined[:rows, :] = shared[...]
    joined[rows:, :] = split[...]


def combine_kernel(
    adapters, width, state, everyone, picks, lead, tail, unit, down, head, merge, slots, held
):
    step = pl.program_id(0)
    count = everyone.shape[0]

    @pl.when(step == 0)
    def _():
        for d in range(count):
            slots[d] = jnp.max(picks[d].astype(F32)).astype(jnp.int32)

    def add_into(target):
        for a in range(adapters):
            target[a] = jnp.zeros(target.shape[1:], F32)
        for d in range(count):
            target[slots[d]] += everyone[d].astype(F32)

    def write(first, blocks, target):
        @pl.when((step >= first) & (step < first + blocks))
        def _():
            add_into(target.at[0])

    write(0, 5, lead)
    write(5, 2, tail)
    write(7, 2, unit)
    write(9, 1, down)

    @pl.when(step == 10)
    def _():
        add_into(held)
        for a in range(adapters):
            for j in range(3):
                head[j, a] = held[a, :, j * width : (j + 1) * width]
            merge[a] = held[a, :, 3 * width :]


class AdapterSums:
    def __init__(self, line, shared, split, slabs):
        rank, full = shared[0].shape[1:]
        width = full // slabs
        self.line, self.rank, self.full, self.width = line, rank, full, width
        slab = (7 * rank, width)
        shapes = ((2, *slab), slab, slab, (5 * rank, full))
        arrays = (*shared, *split)
        far, beside, self.own, self.split = line.call(
            functools.partial(wire_kernel, len(shared)),
            "wire",
            (1,),
            arrays,
            [whole(x) for x in arrays],
            tuple(jax.ShapeDtypeStruct(shape, BF16) for shape in shapes),
            tuple(out_whole(shape) for shape in shapes),
            [pltpu.VMEM((7 * rank, full), BF16)],
        )
        self.slab_sum = SlabSum(line, (far, beside, self.own))

    def cross(self):
        self.slab_sum.cross()

    def spread(self):
        terms = self.slab_sum.terms
        own = self.line.call(
            own_kernel,
            "own",
            (1,),
            terms,
            [whole(x) for x in terms],
            jax.ShapeDtypeStruct(self.own.shape, BF16),
            out_whole(self.own.shape),
        )
        self.parts = spread(own, "pair")

    def join(self):
        shape = (12 * self.rank, self.full)
        sent = self.line.call(
            functools.partial(join_kernel, len(self.parts)),
            "join",
            (1,),
            (*self.parts, self.split),
            [ANY] * len(self.parts) + [whole(self.split)],
            jax.ShapeDtypeStruct(shape, BF16),
            out_whole(shape),
            [pltpu.VMEM((7 * self.rank, self.full), BF16), pltpu.SemaphoreType.DMA((4,))],
        )
        self.everyone = lax.all_gather(sent, "dp", axis=0, tiled=False)

    def combine(self, adapters):
        count = self.everyone.shape[0]
        rank, full, width = self.rank, self.full, self.width

        def sums(first, blocks):
            return pl.BlockSpec(
                (1, adapters, rank, full),
                lambda i, s: (jnp.clip(i - first, 0, blocks - 1), 0, 0, 0),
            )

        def shape(*dims):
            return jax.ShapeDtypeStruct(dims, F32)

        return self.line.call(
            functools.partial(combine_kernel, adapters, width),
            "combine",
            (11,),
            (self.everyone, self.everyone),
            [
                pl.BlockSpec((count, rank, full), lambda i, s: (0, i, 0)),
                pl.BlockSpec((count, rank, 128), lambda i, s: (0, 11, 0)),
            ],
            (
                shape(5, adapters, rank, full),
                shape(2, adapters, rank, full),
                shape(2, adapters, rank, full),
                shape(1, adapters, rank, full),
                shape(3, adapters, rank, width),
                shape(adapters, rank, width),
            ),
            (
                sums(0, 5),
                pl.BlockSpec(
                    (1, adapters, rank, full), lambda i, s: (jnp.where(i < 6, 1, 0), 0, 0, 0)
                ),
                sums(7, 2),
                sums(9, 1),
                out_whole((3, adapters, rank, width)),
                out_whole((adapters, rank, width)),
            ),
            [pltpu.SMEM((count,), jnp.int32), pltpu.VMEM((adapters, rank, full), F32)],
        )


def on_device(
    slabs,
    tokens,
    cotangent,
    norm_gains,
    query_key_value_matrix,
    output_matrix,
    gate_up_matrix,
    down_matrix,
    lead_factors,
    head_factors,
    unit_factors,
    merge_factors,
    down_factors,
    tail_factors,
    doc_ids,
    keep_mask,
    adapter_pick,
):
    length = tokens.shape[1]
    rows = length // CHUNKS
    chosen = adapter_pick[0, 0]
    state = jnp.stack([lax.axis_index("tensor").astype(jnp.int32), chosen])
    line = Line(state)
    gains = norm_gains.astype(F32)
    lead = jnp.swapaxes(lead_factors, 2, 3)
    merge = jnp.swapaxes(merge_factors, 1, 2)
    down = jnp.swapaxes(down_factors, 1, 2)
    cosine, sine = rope_tables(length)
    doc_column = doc_ids.reshape(length, 1)

    def cut(array, c):
        return array[c * rows : (c + 1) * rows]

    own_tokens = [cut(tokens[0], c) for c in range(CHUNKS)]
    token_parts = spread(tokens[0], MODES["tok"])
    own_cots = [cut(cotangent[0], c) for c in range(CHUNKS)]
    cot_parts = spread(cotangent[0], MODES["cot"])

    def project_chunk(c, after=()):
        return project(
            line,
            token_parts,
            c,
            gains,
            lead,
            query_key_value_matrix,
            head_factors,
            cut(cosine, c),
            cut(sine, c),
            after,
        )

    def attend_chunk(c, qkvs, after=()):
        return attend(
            line,
            qkvs,
            c,
            doc_column,
            doc_ids,
            keep_mask,
            output_matrix,
            merge,
            tail_factors,
            slabs,
            MODES["branch"][c],
            after,
        )

    def feed_chunk(c, parts, after=()):
        return feed_forward(
            line,
            parts,
            cot_parts,
            c,
            gains,
            lead,
            gate_up_matrix,
            down_matrix,
            unit_factors,
            down,
            tail_factors,
            (MODES["feed"][c], MODES["back"][c]),
            after,
        )

    def attend_back_chunk(c, parts, after=()):
        return attend_back(
            line,
            parts,
            qkvs[: c + 1],
            c,
            doc_column,
            doc_ids,
            keep_mask,
            attended[c],
            output_matrix,
            merge,
            tail_factors,
            after,
        )

    def project_back_chunk(c, after=()):
        normed, _, scale = saved[c]
        return project_back(
            line,
            gradients,
            backs,
            c,
            query_key_value_matrix,
            lead,
            gains,
            normed,
            scale,
            slabs,
            MODES["last"][c],
            after,
        )

    adapters = lead_factors.shape[1]
    qkv0, *saved0 = project_chunk(0)
    attended0, *branch0 = attend_chunk(0, [qkv0])
    branch0 = SlabSum(line, branch0)
    qkv1, *saved1 = project_chunk(1)
    qkvs, saved = [qkv0, qkv1], [saved0, saved1]
    branch0.cross()
    attended1, *branch1 = attend_chunk(1, qkvs)
    attended = [attended0, attended1]
    branch1 = SlabSum(line, branch1)
    hidden0, rounded0 = branch0.finish(own_tokens[0])
    hidden_parts0 = spread(rounded0, MODES["hidden"][0])
    branch1.cross()
    hidden1, rounded1 = branch1.finish(own_tokens[1])
    hidden_parts1 = spread(rounded1, MODES["hidden"][1])
    feed0, back0, unit_grads0 = feed_chunk(0, hidden_parts0)
    back0 = SlabSum(line, back0)
    feed0 = SlabSum(line, feed0)
    feed1, back1, unit_grads1 = feed_chunk(1, hidden_parts1)
    back1 = SlabSum(line, back1)
    grad0, rounded0 = back0.finish(own_cots[0], (feed0.received,))
    grad_parts0 = spread(rounded0, MODES["grad"][0])
    back1.cross()
    grad1, rounded1 = back1.finish(own_cots[1])
    grad_parts1 = spread(rounded1, MODES["grad"][1])
    query_grad0, key_grad0, value_grad0, *merge_grads0 = attend_back_chunk(0, grad_parts0)
    feed0.cross()
    feed1 = SlabSum(line, relay(line, feed1, (grad_parts1[0],)))
    query_grad1, key_grad1, value_grad1, *merge_grads1 = attend_back_chunk(1, grad_parts1)
    gradients, backs, head_grad, lead_grad = head_back(
        line,
        (query_grad0, query_grad1),
        (key_grad0, key_grad1),
        (value_grad0, value_grad1),
        saved,
        head_factors,
        cosine,
        sine,
    )
    sums = AdapterSums(
        line,
        (
            lead_grad,
            unit_grads0[2],
            unit_grads1[2],
            unit_grads0[3],
            unit_grads1[3],
            merge_grads0[1],
            merge_grads1[1],
        ),
        (
            unit_grads0[0],
            unit_grads1[0],
            unit_grads0[1],
            unit_grads1[1],
            head_grad,
            jnp.stack([merge_grads0[0], merge_grads1[0]]),
        ),
        slabs,
    )
    sums.cross()
    sums.spread()
    last1 = SlabSum(line, project_back_chunk(1, tuple(feed1.terms)))
    sums.join()
    last0 = SlabSum(line, project_back_chunk(0))
    last1.cross()
    last0.cross()
    lead_all, tail_all, unit_all, down_all, head_all, merge_all = sums.combine(adapters)
    _, out0 = feed0.finish(hidden0)
    layer_out = feed1.finish_beside(hidden1, out0, 1)
    _, tokens_grad1 = last1.finish(grad1)
    tokens_grad = last0.finish_beside(grad0, tokens_grad1, 0)
    return (
        layer_out[None],
        tokens_grad[None],
        jnp.swapaxes(lead_all, 2, 3),
        head_all,
        unit_all,
        jnp.swapaxes(merge_all, 1, 2),
        jnp.swapaxes(down_all[0], 1, 2),
        tail_all,
    )


def solution(mesh):
    return jax.shard_map(
        functools.partial(on_device, mesh.shape["tensor"]),
        mesh=mesh,
        in_specs=(
            P("dp", None, "tensor"),
            P("dp", None, "tensor"),
            P(),
            P(None, None, "tensor"),
            P("tensor", None),
            P(None, None, "tensor"),
            P("tensor", None),
            P(),
            P(None, None, None, "tensor"),
            P(None, None, None, "tensor"),
            P(None, "tensor", None),
            P(None, "tensor", None),
            P(),
            P("dp", None),
            P("dp", None),
            P("dp", None),
        ),
        out_specs=(
            P("dp", None, "tensor"),
            P("dp", None, "tensor"),
            P(),
            P(None, None, None, "tensor"),
            P(None, None, None, "tensor"),
            P(None, "tensor", None),
            P(None, "tensor", None),
            P(),
        ),
        check_vma=False,
    )
```
